256 devices in a mesh: dp: 32 (over x, y, core), mp: 8 (over z).
Axes of the slice: x: 4, y: 4, z: 8, core: 2. Of those that a mesh axis runs over, the one named last changes fastest.
Arguments:
- queries: bfloat16 [8192, 4096], P('dp', 'mp'), may hold values from -6 to 6
- enc_rows: bfloat16 [4096, 4096], P('dp', 'mp'), may hold values from -6 to 6
- key_weight: bfloat16 [4096, 4096], P(None, 'mp'), may hold values from -0.09375 to 0.09375
- value_weight: bfloat16 [4096, 4096], P(None, 'mp'), may hold values from -0.09375 to 0.09375
- enc_len: int32 [32, 32], P('dp'), may hold values from 1 to 16, 128 in all within a row
- dec_len: int32 [32, 32], P('dp'), may hold values from 1 to 32, 256 in all within a row
- route: int32 [32, 32], P('dp'), may hold values from 0 to 31, each once within a row
- out_grad: bfloat16 [8192, 4096], P('dp', 'mp'), may hold values from -6 to 6
Outputs:
- attended: bfloat16 [8192, 4096], P('dp', 'mp')
- query_grad: bfloat16 [8192, 4096], P('dp', 'mp')
- enc_grad: bfloat16 [4096, 4096], P('dp', 'mp')
- key_weight_grad: float32 [4096, 4096], P('dp', 'mp')
- value_weight_grad: float32 [4096, 4096], P('dp', 'mp')
The draws below stay inside these ranges and needn't reach their ends.
Inputs may be any that keep to these rules, and one draw needn't show every extreme that they name: Every row of enc_len sums to 128, and its largest entry is exactly 16. Every row of dec_len sums to 256, and its largest entry is exactly 32. Every row of route is a permutation of the data shards, so each decoder shard receives exactly one example from each shard.
All inputs are finite; a program needn't handle non-finite values.
Results may differ from the reference program's by a relative error of at most 0.013.
Values may be sent and summed in bfloat16 or wider, within the bound.
A program may use at most 128 MiB of HBM per device.

```python
import math
import jax
import jax.numpy as jnp
import numpy as np
from jax import lax

D = 4096
HEADS = 16
HD = 256
ENC_DEV = 128
DEC_DEV = 256
ENC_MOST = 16
DEC_MOST = 32
ENC_TOTAL = 4096
DEC_TOTAL = 8192
N_DP = 32


def draw_queries(key, part):
    key = jax.random.fold_in(key, 11)
    shape = (DEC_TOTAL, HEADS * HD)
    draws = jnp.clip(jax.random.normal(key, shape, jnp.float32), -6.0, 6.0)
    return draws.astype(jnp.bfloat16)


def with_spikes(values, rng, source, target, parts, factor):
    owner, partner = [(jnp.arange(values.shape[dim]) // (values.shape[dim] // parts)).reshape([-1 if axis == dim else 1 for axis in range(values.ndim)]) for dim in (source, target)]
    chosen = jax.random.permutation(rng, parts)[partner]
    strong = (owner == chosen) | (owner == (partner + parts // 2) % parts)
    return jnp.where(strong, factor * values, values)


def steps_of(own_key, dims, cuts, smallest, largest):
    factor_of = 1.0
    for axis_at, shards_of in cuts:
        steps = jax.random.uniform(jax.random.fold_in(jax.random.fold_in(own_key, 6), axis_at), (shards_of,), jnp.float32, smallest / len(cuts), largest / len(cuts))
        factor_of = factor_of * jnp.repeat(jnp.exp(steps), dims[axis_at] // shards_of).reshape((-1,) + (1,) * (len(dims) - 1 - axis_at))
    return factor_of


def split_up(count, total, bound, lean):
    portions = [(1 << 20) // math.isqrt(rank ** lean) + 1 for rank in range(2, count + 1)]
    surplus, counts = total - bound - (count - 1), [1] * (count - 1)
    while surplus > 0:
        free = [i for i in range(count - 1) if counts[i] < bound]
        whole, left = sum([portions[i] for i in free]), surplus
        for i in free:
            more = min(bound - counts[i], max(1, left * portions[i] // whole), surplus)
            counts[i] = counts[i] + more
            surplus = surplus - more
    return np.array([bound] + counts)


def uneven(rng, count, total, bound, skew):
    if count == 2:
        one = jax.random.randint(rng, (), max(1, total - bound), min(bound, total - 1) + 1)
        return jnp.stack([one, total - one])
    tallies = jnp.asarray(split_up(count, total, bound, skew), jnp.int32)
    pairs = (count - 1) // 2
    giver, sink = tallies[1:1 + 2 * pairs:2], tallies[2:2 + 2 * pairs:2]
    slack = jnp.minimum(giver - 1, bound - sink)
    moved = jax.random.randint(jax.random.fold_in(rng, 1), (pairs,), 0, 1 << 20) % (slack + 1)
    tallies = tallies.at[1:1 + 2 * pairs:2].set(giver - moved).at[2:2 + 2 * pairs:2].set(sink + moved)
    return tallies[jax.random.permutation(jax.random.fold_in(rng, 2), count)]


def centred(key, dims, spread, reach, cuts=(), kind=jnp.bfloat16):
    result = jax.random.normal(key, dims, jnp.float32) * spread
    if len(cuts) > 0:
        result = steps_of(key, dims, cuts, -0.22, 0.18) * result
    return jnp.clip(result, min=-reach, max=reach).astype(kind)


def heavy_noise(own_key, extent, spread, limit, split, heavy, kind=jnp.bfloat16):
    drawn = spread * jax.random.normal(own_key, extent, jnp.float32)
    if split:
        drawn = drawn * steps_of(own_key, extent, split, -0.22, 0.18)
    return jnp.clip(with_spikes(drawn, jax.random.fold_in(own_key, 3), *heavy), -limit, limit).astype(kind)


def setup_inputs(seed: int = 0) -> dict:
    streams_of = jax.random.split(jax.random.key(seed), 9)
    queries = draw_queries(jax.random.fold_in(streams_of[8], 71), 0)
    enc_rows = heavy_noise(streams_of[1], (ENC_TOTAL, D), 1.0, 6.0, ((0, 32), (1, 8)), (0, 1, 32, 2.75))
    key_weight = centred(streams_of[2], (D, HEADS * HD), D ** -0.5, 0.09375, ((1, 8),))
    value_weight = centred(streams_of[3], (D, HEADS * HD), D ** -0.5, 0.09375, ((1, 8),))
    enc_len = jax.vmap(lambda own: uneven(own, N_DP, ENC_DEV, ENC_MOST, 2))(jax.random.split(streams_of[4], N_DP)).reshape((N_DP, N_DP)).astype(jnp.int32)
    dec_len = jax.vmap(lambda own: uneven(own, N_DP, DEC_DEV, DEC_MOST, 2))(jax.random.split(streams_of[5], N_DP)).reshape((N_DP, N_DP)).astype(jnp.int32)
    route = jax.vmap(lambda own: jax.random.permutation(own, N_DP))(jax.random.split(streams_of[6], N_DP)).reshape((N_DP, N_DP)).astype(jnp.int32)
    out_grad = centred(streams_of[7], (DEC_TOTAL, HEADS * HD), 1.0, 6.0, ((0, 32), (1, 8)))
    return {"queries": queries, "enc_rows": enc_rows, "key_weight": key_weight, "value_weight": value_weight, "enc_len": enc_len, "dec_len": dec_len, "route": route, "out_grad": out_grad}


def attend(q_rows, g_rows, key_buf, val_buf, key_live, dec_lens):
    rows = q_rows.shape[0]
    keys_n = key_buf.shape[0]
    heads = q_rows.shape[1] // HD
    scale = HD ** -0.5
    query_h = q_rows.reshape(rows, heads, HD).astype(jnp.float32)
    grad_h = g_rows.reshape(rows, heads, HD).astype(jnp.float32)
    key_h = key_buf.reshape(keys_n, heads, HD).astype(jnp.float32)
    val_h = val_buf.reshape(keys_n, heads, HD).astype(jnp.float32)
    dec_ends = jnp.cumsum(dec_lens, dtype=jnp.int32)
    dec_pos = jnp.arange(rows, dtype=jnp.int32)
    dec_source = jnp.sum((dec_ends[None, :] <= dec_pos[:, None]).astype(jnp.int32), axis=1, dtype=jnp.int32)
    key_source = jnp.arange(keys_n, dtype=jnp.int32) // ENC_MOST
    allowed = (dec_source[:, None] == key_source[None, :]) & key_live[None, :]
    scores = jnp.einsum("qhd,khd->hqk", query_h, key_h) * scale
    scores = jnp.where(allowed[None], scores, -jnp.inf)
    top = jnp.max(scores, axis=-1, keepdims=True)
    expo = jnp.exp(scores - top)
    probs = expo / jnp.sum(expo, axis=-1, keepdims=True)
    weights = probs.astype(jnp.bfloat16)
    attended = jnp.einsum("hqk,khd->qhd", weights.astype(jnp.float32), val_h).astype(jnp.bfloat16)
    dweights = jnp.einsum("qhd,khd->hqk", grad_h, val_h)
    delta = jnp.sum(probs * dweights, axis=-1, keepdims=True)
    dscores = (probs * (dweights - delta) * scale).astype(jnp.bfloat16).astype(jnp.float32)
    query_grad = jnp.einsum("hqk,khd->qhd", dscores, key_h).astype(jnp.bfloat16)
    key_grad = jnp.einsum("hqk,qhd->khd", dscores, query_h).astype(jnp.bfloat16)
    value_grad = jnp.einsum("hqk,qhd->khd", weights.astype(jnp.float32), grad_h).astype(jnp.bfloat16)
    width = heads * HD
    return (attended.reshape(rows, width), query_grad.reshape(rows, width),
            key_grad.reshape(keys_n, width), value_grad.reshape(keys_n, width))


def reference(queries, enc_rows, key_weight, value_weight, enc_len, dec_len, route, out_grad):
    width = HEADS * HD
    keys = jnp.dot(enc_rows, key_weight, preferred_element_type=jnp.float32).astype(jnp.bfloat16)
    values = jnp.dot(enc_rows, value_weight, preferred_element_type=jnp.float32).astype(jnp.bfloat16)
    starts = jnp.cumsum(enc_len, axis=1, dtype=jnp.int32) - enc_len
    shards = jnp.arange(N_DP, dtype=jnp.int32)
    pick = route[:, :, None] == shards[None, None, :]
    start_st = jnp.sum(jnp.where(pick, starts[:, :, None], 0), axis=1, dtype=jnp.int32)
    len_st = jnp.sum(jnp.where(pick, enc_len[:, :, None], 0), axis=1, dtype=jnp.int32)
    offsets = jnp.arange(ENC_MOST, dtype=jnp.int32)
    live = offsets[None, None, :] < len_st.T[:, :, None]
    index = shards[None, :, None] * ENC_DEV + start_st.T[:, :, None] + offsets[None, None, :]
    index = jnp.where(live, index, 0).astype(jnp.int32).reshape(N_DP, N_DP * ENC_MOST)
    live = live.reshape(N_DP, N_DP * ENC_MOST)

    def one_shard(items):
        rows_at, live_at, q_rows, g_rows, lens = items
        key_buf = jnp.where(live_at[:, None], keys[rows_at], jnp.zeros((), jnp.bfloat16))
        val_buf = jnp.where(live_at[:, None], values[rows_at], jnp.zeros((), jnp.bfloat16))
        return attend(q_rows, g_rows, key_buf, val_buf, live_at, lens)

    attended, query_grad, key_slots, value_slots = lax.map(
        one_shard, (index, live, queries.reshape(N_DP, DEC_DEV, width),
                    out_grad.reshape(N_DP, DEC_DEV, width), dec_len))
    flat_index = index.reshape(-1)
    flat_live = live.reshape(-1, 1)
    key_grad = jnp.zeros((ENC_TOTAL, width), jnp.float32).at[flat_index].add(
        jnp.where(flat_live, key_slots.reshape(-1, width).astype(jnp.float32), 0.0)).astype(jnp.bfloat16)
    value_grad = jnp.zeros((ENC_TOTAL, width), jnp.float32).at[flat_index].add(
        jnp.where(flat_live, value_slots.reshape(-1, width).astype(jnp.float32), 0.0)).astype(jnp.bfloat16)
    contract_cols = (((1,), (1,)), ((), ()))
    enc_grad = (lax.dot_general(key_grad, key_weight, contract_cols, preferred_element_type=jnp.float32)
                + lax.dot_general(value_grad, value_weight, contract_cols, preferred_element_type=jnp.float32)).astype(jnp.bfloat16)
    contract_rows = (((0,), (0,)), ((), ()))
    key_weight_grad = lax.dot_general(enc_rows, key_grad, contract_rows, preferred_element_type=jnp.float32)
    value_weight_grad = lax.dot_general(enc_rows, value_grad, contract_rows, preferred_element_type=jnp.float32)
    return (attended.reshape(DEC_TOTAL, width), query_grad.reshape(DEC_TOTAL, width),
            enc_grad, key_weight_grad, value_weight_grad)
```

```python
import functools

import jax
import jax.numpy as jnp
from jax import lax
from jax.experimental import pallas as pl
from jax.experimental.pallas import tpu as pltpu
from jax.sharding import PartitionSpec as P

HD = 256
ROWS = 128
DEC = 256
SLOT = 16
NDP = 32
NZ = 8
W2 = 512
DEAD = 65536.0
MESH = pl.DeviceIdType.MESH
BF = jnp.bfloat16
F32 = jnp.float32


def mm(a, b):
    return lax.dot_general(a, b, (((1,), (0,)), ((), ())), preferred_element_type=F32)


def mm_nt(a, b):
    return lax.dot_general(a, b, (((1,), (1,)), ((), ())), preferred_element_type=F32)


def mm_tn(a, b):
    return lax.dot_general(a, b, (((0,), (0,)), ((), ())), preferred_element_type=F32)


def iota(shape, dim):
    return lax.broadcasted_iota(jnp.int32, shape, dim)


def column_of(row, n):
    here = iota((n, n), 1)
    there = iota((n, n), 0)
    wide = jnp.broadcast_to(row, (n, n))
    col = jnp.sum(jnp.where(here == there, wide, 0.0), axis=1, keepdims=True)
    before = jnp.sum(jnp.where(here < there, wide, 0.0), axis=1, keepdims=True)
    return col, before


def kernel(
    q_hbm, enc_hbm, kw_hbm, vw_hbm, enc_len, dec_len, route, og_hbm,
    att_hbm, qg_hbm, eg_hbm, kwg_hbm, vwg_hbm,
    e_v, et_v, kw_v, vw_v, q_v, og_v, acc, oh_v,
    slots, kvr, gs, gr, gsend, gl, el, ps, cr, dx, rs_s, rs_r,
    att_v, qg_v, eg_v, wg_v,
    enc_sem, w_sem, q_sem, z_send, z_recv, el_send, el_recv,
    kv_send, kv_recv, g_send, g_recv, gl_send, gl_recv, c_send, c_recv,
    rs_send, rs_recv, out_sem,
):
    d = lax.axis_index("dp")
    z = lax.axis_index("mp")
    x = d // 8
    y = (d // 2) % 4
    c = d % 2
    right = (d, (z + 1) % NZ)
    left = (d, (z + NZ - 1) % NZ)
    ring = (right, left)

    def chunk_at(n):
        off = jnp.where(n % 2 == 1, NZ - (n + 1) // 2, n // 2)
        return (z + off) % NZ

    for b in range(4):
        pltpu.make_async_copy(
            enc_hbm.at[:, pl.ds(b * 128, 128)], e_v.at[z * 4 + b], enc_sem
        ).start()

    def w_copy(zc, kv):
        src, dst = ((kw_hbm, kw_v), (vw_hbm, vw_v))[kv]
        return pltpu.make_async_copy(
            src.at[pl.ds(pl.multiple_of(zc * W2, W2), W2), :], dst.at[zc], w_sem.at[zc, kv]
        )

    def load_w(n, carry):
        zc = chunk_at(n)
        w_copy(zc, 0).start()
        w_copy(zc, 1).start()
        return carry

    lax.fori_loop(0, NZ, load_w, 0)
    q_copy = pltpu.make_async_copy(q_hbm, q_v, q_sem.at[0])
    og_copy = pltpu.make_async_copy(og_hbm, og_v, q_sem.at[1])
    q_copy.start()
    og_copy.start()

    barrier = pltpu.get_barrier_semaphore()
    for peer in ring:
        pl.semaphore_signal(barrier, inc=1, device_id=peer, device_id_type=MESH)

    def greet(i, carry):
        pl.semaphore_signal(barrier, inc=1, device_id=((d + i) % NDP, z), device_id_type=MESH)
        return carry

    lax.fori_loop(1, NDP, greet, 0)

    lens_col, starts_col = column_of(enc_len[...].astype(F32), NDP)
    route_col, _ = column_of(route[...].astype(F32), NDP)
    pos = iota((NDP, ROWS), 1).astype(F32)
    inside = (pos >= starts_col) & (pos < starts_col + lens_col)
    dest = jnp.sum(
        jnp.where(inside, route_col * SLOT + pos - starts_col, 0.0), axis=0, keepdims=True
    )
    hot = iota((NDP * SLOT, ROWS), 0).astype(F32) == dest
    hot_f = jnp.where(hot, 1.0, 0.0)
    oh_v[...] = hot_f.astype(BF)

    pl.semaphore_wait(barrier, NDP + 1)
    pltpu.make_async_copy(e_v.at[pl.ds(0, 4)], e_v.at[pl.ds(z * 4, 4)], enc_sem).wait()

    def z_copy(direction, step, part):
        back = step - 1
        zc = (z + NZ - back) % NZ if direction == 0 else (z + back) % NZ
        at = pl.ds(zc * 4 + 2 * part, 2)
        return pltpu.make_async_remote_copy(
            src_ref=e_v.at[at],
            dst_ref=e_v.at[at],
            send_sem=z_send.at[direction, step - 1, part],
            recv_sem=z_recv.at[direction, step - 1, part],
            device_id=ring[direction],
            device_id_type=MESH,
        )

    for part in range(2):
        for direction in range(2):
            z_copy(direction, 1, part).start()

    def to_line(src, dst, device, here):
        @pl.when(here)
        def _():
            pltpu.make_async_copy(src, dst, el_recv).start()

        @pl.when(jnp.logical_not(here))
        def _():
            pltpu.make_async_remote_copy(
                src_ref=src, dst_ref=dst, send_sem=el_send, recv_sem=el_recv,
                device_id=device, device_id_type=MESH,
            ).start()

    acc[...] = jnp.zeros_like(acc)

    def process(zc):
        blocks = [e_v[zc * 4 + b] for b in range(4)]
        rows = jnp.concatenate(blocks, axis=1)
        w_copy(zc, 0).wait()
        w_copy(zc, 1).wait()
        acc[:, :W2] += mm(rows, kw_v[zc])
        acc[:, W2:] += mm(rows, vw_v[zc])
        for b in range(4):
            et_v[zc * 4 + b] = blocks[b].T
        xc = zc // 2
        half = zc % 2
        to_line(
            et_v.at[pl.ds(zc * 4, 4)], el.at[x * 2 + c, pl.ds(half * 4, 4)],
            (xc * 8 + y * 2, z), (xc == x) & (c == 0),
        )
        for j in range(2):
            yc = half * 2 + j
            to_line(
                et_v.at[pl.ds(zc * 4 + 2 * j, 2)], el.at[y * 2 + c, pl.ds(xc * 2, 2)],
                (x * 8 + yc * 2 + 1, z), (yc == y) & (c == 1),
            )

    process(z)

    def gather_step(k, carry):
        for part in range(2):
            for direction in range(2):
                z_copy(direction, k, part).wait_recv()
                if part == direction:
                    z_copy(direction, k + 1, part).start()
                else:
                    @pl.when(k < 3)
                    def _():
                        z_copy(direction, k + 1, part).start()
        process((z + NZ - k) % NZ)
        process((z + k) % NZ)
        return carry

    lax.fori_loop(1, 4, gather_step, 0)
    z_copy(0, 4, 0).wait_recv()
    z_copy(1, 4, 1).wait_recv()
    process((z + 4) % NZ)

    def exchange(src, dst, send_sem, recv_sem, h):
        mine = pl.ds(pl.multiple_of(d * SLOT, SLOT), SLOT)
        pltpu.make_async_copy(src.at[h, mine], dst.at[h, mine], recv_sem.at[h]).start()

        def send(i, carry):
            o = (i * 11) % NDP
            t = ((x + o // 8) % 4) * 8 + ((y + (o // 2) % 4) % 4) * 2 + (c + o % 2) % 2
            pltpu.make_async_remote_copy(
                src_ref=src.at[h, pl.ds(pl.multiple_of(t * SLOT, SLOT), SLOT)],
                dst_ref=dst.at[h, mine],
                send_sem=send_sem.at[h],
                recv_sem=recv_sem.at[h],
                device_id=(t, z),
                device_id_type=MESH,
            ).start()
            return carry

        lax.fori_loop(1, NDP, send, 0)

    def drained(buf, sem):
        pltpu.make_async_copy(buf, buf, sem).wait()

    most = pl.ds(0, (NDP - 1) * SLOT)
    hot_b = oh_v[...]
    dead = jnp.sum(hot_b.astype(F32), axis=1, keepdims=True) < 0.5
    for h in range(2):
        cols = pl.ds(h * HD, HD)
        keys = mm(hot_b, acc[:, cols].astype(BF))
        slots[h, :, :HD] = jnp.where(dead, DEAD, keys).astype(BF)
        slots[h, :, HD:] = mm(hot_b, acc[:, pl.ds(W2 + h * HD, HD)].astype(BF)).astype(BF)
        exchange(slots, kvr, kv_send, kv_recv, h)

    n_keys = NDP * SLOT
    dec_col, dec_before = column_of(dec_len[...].astype(F32), NDP)
    same = iota((NDP, n_keys), 1) // SLOT == iota((NDP, n_keys), 0)
    first = jnp.sum(jnp.where(same, dec_before, 0.0), axis=0, keepdims=True)
    last = jnp.sum(jnp.where(same, dec_before + dec_col, 0.0), axis=0, keepdims=True)
    row = iota((DEC, n_keys), 0).astype(F32)
    own = (row >= first) & (row < last)
    q_copy.wait()
    og_copy.wait()
    for h in range(2):
        cols = pl.ds(h * HD, HD)
        drained(kvr.at[h], kv_recv.at[h])
        q = q_v[:, cols]
        g = og_v[:, cols]
        k = kvr[h, :, :HD]
        v = kvr[h, :, HD:]
        total = mm_nt(jnp.ones((16, HD), BF), k)[:1]
        allowed = own & (total < 4.0e6)
        s = jnp.where(allowed, mm_nt(q, k) * (HD ** -0.5), -1e30)
        top = jnp.max(s, axis=1, keepdims=True)
        expo = jnp.exp(s - top)
        probs = expo * (1.0 / jnp.sum(expo, axis=1, keepdims=True))
        weights = probs.astype(BF)
        dw = mm_nt(g, v)
        delta = jnp.sum(probs * dw, axis=1, keepdims=True)
        ds = (probs * (dw - delta) * (HD ** -0.5)).astype(BF)
        gs[h, :, :HD] = mm_tn(ds, q).astype(BF)
        gs[h, :, HD:] = mm_tn(weights, g).astype(BF)
        exchange(gs, gr, g_send, g_recv, h)
        att_v[:, cols] = mm(weights, v).astype(BF)
        qg_v[:, cols] = mm(ds, k).astype(BF)
    att_out = pltpu.make_async_copy(att_v, att_hbm, out_sem.at[0])
    qg_out = pltpu.make_async_copy(qg_v, qg_hbm, out_sem.at[1])
    att_out.start()
    qg_out.start()

    def spread(h):
        def one(kv, i):
            if kv == 0:
                t = ((x + i) % 4) * 8 + y * 2
                at = x * 2 + c
            else:
                t = x * 8 + ((y + i) % 4) * 2 + 1
                at = y * 2 + c
            src = gsend.at[h, kv]
            dst = gl.at[h, pl.ds(pl.multiple_of(at * ROWS, ROWS), ROWS)]

            def far():
                pltpu.make_async_remote_copy(
                    src_ref=src, dst_ref=dst, send_sem=gl_send.at[h], recv_sem=gl_recv.at[h],
                    device_id=(t, z), device_id_type=MESH,
                ).start()

            if i > 0:
                far()
            else:
                pl.when(c != kv)(far)

                @pl.when(c == kv)
                def _():
                    pltpu.make_async_copy(src, dst, gl_recv.at[h]).start()

        for i in (2, 1, 3, 0):
            one(0, i)
            one(1, i)

    def unpack(h):
        drained(gr.at[h], g_recv.at[h])
        rows = mm_tn(oh_v[...], gr[h]).astype(BF)
        gsend[h, 0] = rows[:, :HD]
        gsend[h, 1] = rows[:, HD:]
        spread(h)

    def back(h, i):
        zc = i // 2
        at = pl.ds(pl.multiple_of((i % 2) * HD, HD), HD)
        cols = pl.ds(h * HD, HD)
        return mm_nt(gsend[h, 0], kw_v[zc, at, cols]) + mm_nt(gsend[h, 1], vw_v[zc, at, cols])

    def partial_blocks(h):
        drained(gl.at[h], gl_recv.at[h])

        def block(b, carry):
            lhs = jnp.concatenate([el[j, b] for j in range(8)], axis=1)
            ps[h, b] = mm(lhs, gl[h]).astype(BF)
            t = jnp.where(c == 0, x * 8 + b, (b // 2) * 8 + y * 2 + b % 2)
            dst = cr.at[h, c, jnp.where(c == 0, y, x)]

            @pl.when(t == d)
            def _():
                pltpu.make_async_copy(ps.at[h, b], dst, c_recv.at[h]).start()

            @pl.when(t != d)
            def _():
                pltpu.make_async_remote_copy(
                    src_ref=ps.at[h, b], dst_ref=dst, send_sem=c_send.at[h], recv_sem=c_recv.at[h],
                    device_id=(t, z), device_id_type=MESH,
                ).start()

            return carry

        lax.fori_loop(0, 8, block, 0)

    unpack(0)

    def back_first(i, carry):
        dx[i] = back(0, i)
        return carry

    lax.fori_loop(0, 2 * NZ, back_first, 0)
    drained(el, el_recv)
    partial_blocks(0)
    unpack(1)

    def rs_copy(direction, step, part):
        return pltpu.make_async_remote_copy(
            src_ref=rs_s.at[direction, step - 1, part],
            dst_ref=rs_r.at[direction, step - 1, part],
            send_sem=rs_send.at[direction, step - 1, part],
            recv_sem=rs_recv.at[direction, step - 1, part],
            device_id=ring[direction],
            device_id_type=MESH,
        )

    def rs_step(step):
        order = ((0, 0), (1, 1)) if step == 1 else ((0, 0), (1, 1), (0, 1), (1, 0))
        for direction, part in order:
            far = 5 - step
            zc = (z + far) % NZ if direction == 0 else (z + NZ - far) % NZ
            i = zc * 2 + part
            term = dx[i] + back(1, i)
            if step >= 3 or (step == 2 and part == direction):
                rs_copy(direction, step - 1, part).wait_recv()
                term = term + rs_r[direction, step - 2, part].astype(F32)
            rs_s[direction, step - 1, part] = term.astype(BF)
            rs_copy(direction, step, part).start()

    rs_step(1)
    partial_blocks(1)
    rs_step(2)
    rs_step(3)
    rs_step(4)

    for h in range(2):
        drained(cr.at[h], c_recv.at[h])
        cols = pl.ds(h * HD, HD)
        for kv in range(2):
            total = cr[h, kv, 0].astype(F32)
            for j in range(1, 4):
                total = total + cr[h, kv, j].astype(F32)
            wg_v[kv, :, cols] = total
    kwg_out = pltpu.make_async_copy(wg_v.at[0], kwg_hbm, out_sem.at[2])
    vwg_out = pltpu.make_async_copy(wg_v.at[1], vwg_hbm, out_sem.at[3])
    kwg_out.start()
    vwg_out.start()
    for part in range(2):
        i = z * 2 + part
        total = dx[i] + back(1, i)
        for direction in range(2):
            rs_copy(direction, 4, part).wait_recv()
            total = total + rs_r[direction, 3, part].astype(F32)
        eg_v[:, pl.ds(part * HD, HD)] = total.astype(BF)
    eg_out = pltpu.make_async_copy(eg_v, eg_hbm, out_sem.at[4])
    eg_out.start()

    for direction in range(2):
        for step in range(1, 5):
            for part in range(2):
                if step < 4 or part == direction:
                    z_copy(direction, step, part).wait_send()
                if step > 1 or part == direction:
                    rs_copy(direction, step, part).wait_send()
    drained(el.at[pl.ds(0, 7)], el_send)
    for h in range(2):
        drained(kvr.at[h, most], kv_send.at[h])
        drained(gr.at[h, most], g_send.at[h])
        drained(gl.at[h, pl.ds(0, 7 * ROWS)], gl_send.at[h])
        drained(ps.at[h, pl.ds(0, 7)], c_send.at[h])
    att_out.wait()
    qg_out.wait()
    kwg_out.wait()
    vwg_out.wait()
    eg_out.wait()


def body(queries, enc_rows, key_weight, value_weight, enc_len, dec_len, route, out_grad):
    any_spec = pl.BlockSpec(memory_space=pl.ANY)
    small = pl.BlockSpec(memory_space=pltpu.VMEM)
    dma = pltpu.SemaphoreType.DMA
    return pl.pallas_call(
        kernel,
        out_shape=(
            jax.ShapeDtypeStruct((DEC, W2), BF),
            jax.ShapeDtypeStruct((DEC, W2), BF),
            jax.ShapeDtypeStruct((ROWS, W2), BF),
            jax.ShapeDtypeStruct((ROWS, W2), F32),
            jax.ShapeDtypeStruct((ROWS, W2), F32),
        ),
        in_specs=[any_spec] * 4 + [small] * 3 + [any_spec],
        out_specs=[any_spec] * 5,
        scratch_shapes=[
            pltpu.VMEM((32, 128, 128), BF),
            pltpu.VMEM((32, 128, 128), BF),
            pltpu.VMEM((NZ, W2, W2), BF),
            pltpu.VMEM((NZ, W2, W2), BF),
            pltpu.VMEM((DEC, W2), BF),
            pltpu.VMEM((DEC, W2), BF),
            pltpu.VMEM((ROWS, 2 * W2), F32),
            pltpu.VMEM((NDP * SLOT, ROWS), BF),
            pltpu.VMEM((2, NDP * SLOT, W2), BF),
            pltpu.VMEM((2, NDP * SLOT, W2), BF),
            pltpu.VMEM((2, NDP * SLOT, W2), BF),
            pltpu.VMEM((2, NDP * SLOT, W2), BF),
            pltpu.VMEM((2, 2, ROWS, HD), BF),
            pltpu.VMEM((2, 8 * ROWS, HD), BF),
            pltpu.VMEM((8, 8, 128, 128), BF),
            pltpu.VMEM((2, 8, 128, HD), BF),
            pltpu.VMEM((2, 2, 4, 128, HD), BF),
            pltpu.VMEM((2 * NZ, ROWS, HD), F32),
            pltpu.VMEM((2, 4, 2, ROWS, HD), BF),
            pltpu.VMEM((2, 4, 2, ROWS, HD), BF),
            pltpu.VMEM((DEC, W2), BF),
            pltpu.VMEM((DEC, W2), BF),
            pltpu.VMEM((ROWS, W2), BF),
            pltpu.VMEM((2, ROWS, W2), F32),
            dma(()),
            dma((NZ, 2)),
            dma((2,)),
            dma((2, 4, 2)),
            dma((2, 4, 2)),
            dma(()),
            dma(()),
            dma((2,)),
            dma((2,)),
            dma((2,)),
            dma((2,)),
            dma((2,)),
            dma((2,)),
            dma((2,)),
            dma((2,)),
            dma((2, 4, 2)),
            dma((2, 4, 2)),
            dma((5,)),
        ],
        compiler_params=pltpu.CompilerParams(
            collective_id=0, has_side_effects=True, vmem_limit_bytes=48 * 1024 * 1024
        ),
    )(queries, enc_rows, key_weight, value_weight, enc_len, dec_len, route, out_grad)


def solution(mesh):
    in_specs = (
        P("dp", "mp"),
        P("dp", "mp"),
        P(None, "mp"),
        P(None, "mp"),
        P("dp", None),
        P("dp", None),
        P("dp", None),
        P("dp", "mp"),
    )
    out_specs = (P("dp", "mp"), P("dp", "mp"), P("dp", "mp"), P("dp", "mp"), P("dp", "mp"))
    return jax.shard_map(body, mesh=mesh, in_specs=in_specs, out_specs=out_specs, check_vma=False)
```

```python
import jax
import jax.numpy as jnp
from jax import lax
from jax.experimental import pallas as pl
from jax.experimental.pallas import tpu as pltpu
from jax.sharding import PartitionSpec as P

HD = 256
ROWS = 128
DEC = 256
SLOT = 16
NDP = 32
NZ = 8
W2 = 512
DEAD = 65536.0
MESH = pl.DeviceIdType.MESH
BF = jnp.bfloat16
F32 = jnp.float32


def mm(a, b):
    return lax.dot_general(a, b, (((1,), (0,)), ((), ())), preferred_element_type=F32)


def mm_nt(a, b):
    return lax.dot_general(a, b, (((1,), (1,)), ((), ())), preferred_element_type=F32)


def mm_tn(a, b):
    return lax.dot_general(a, b, (((0,), (0,)), ((), ())), preferred_element_type=F32)


def iota(shape, dim):
    return lax.broadcasted_iota(jnp.int32, shape, dim)


def column_of(row, n):
    here = iota((n, n), 1)
    there = iota((n, n), 0)
    wide = jnp.broadcast_to(row, (n, n))
    col = jnp.sum(jnp.where(here == there, wide, 0.0), axis=1, keepdims=True)
    before = jnp.sum(jnp.where(here < there, wide, 0.0), axis=1, keepdims=True)
    return col, before


def kernel(
    q_hbm, enc_hbm, kw_hbm, vw_hbm, enc_len, dec_len, route, og_hbm,
    att_hbm, qg_hbm, eg_hbm, kwg_hbm, vwg_hbm,
    e_v, et_v, kw_v, vw_v, q_v, og_v, acc, oh_v,
    slots, kvr, gs, gr, gsend, gl, el, ps, cr, dx, rs_s, rs_r,
    att_v, qg_v, eg_v, wg_v,
    enc_sem, w_sem, q_sem, z_send, z_recv, el_send, el_recv,
    kv_send, kv_recv, g_send, g_recv, gl_send, gl_recv, c_send, c_recv,
    rs_send, rs_recv, out_sem,
):
    d = lax.axis_index("dp")
    z = lax.axis_index("mp")
    x = d // 8
    y = (d // 2) % 4
    c = d % 2
    right = (d, (z + 1) % NZ)
    left = (d, (z + NZ - 1) % NZ)
    ring = (right, left)

    def chunk_at(n):
        off = jnp.where(n % 2 == 1, NZ - (n + 1) // 2, n // 2)
        return (z + off) % NZ

    for b in range(4):
        pltpu.make_async_copy(
            enc_hbm.at[:, pl.ds(b * 128, 128)], e_v.at[z * 4 + b], enc_sem
        ).start()

    def w_copy(zc, kv):
        src, dst = ((kw_hbm, kw_v), (vw_hbm, vw_v))[kv]
        return pltpu.make_async_copy(
            src.at[pl.ds(pl.multiple_of(zc * W2, W2), W2), :], dst.at[zc], w_sem.at[zc, kv]
        )

    def load_w(n, carry):
        zc = chunk_at(n)
        w_copy(zc, 0).start()
        w_copy(zc, 1).start()
        return carry

    lax.fori_loop(0, NZ, load_w, 0)
    q_copy = pltpu.make_async_copy(q_hbm, q_v, q_sem.at[0])
    og_copy = pltpu.make_async_copy(og_hbm, og_v, q_sem.at[1])
    q_copy.start()
    og_copy.start()

    barrier = pltpu.get_barrier_semaphore()
    for peer in ring:
        pl.semaphore_signal(barrier, inc=1, device_id=peer, device_id_type=MESH)

    def greet(i, carry):
        pl.semaphore_signal(barrier, inc=1, device_id=((d + i) % NDP, z), device_id_type=MESH)
        return carry

    lax.fori_loop(1, NDP, greet, 0)

    lens_col, starts_col = column_of(enc_len[...].astype(F32), NDP)
    route_col, _ = column_of(route[...].astype(F32), NDP)
    pos = iota((NDP, ROWS), 1).astype(F32)
    inside = (pos >= starts_col) & (pos < starts_col + lens_col)
    dest = jnp.sum(
        jnp.where(inside, route_col * SLOT + pos - starts_col, 0.0), axis=0, keepdims=True
    )
    hot = iota((NDP * SLOT, ROWS), 0).astype(F32) == dest
    hot_f = jnp.where(hot, 1.0, 0.0)
    oh_v[...] = hot_f.astype(BF)

    pl.semaphore_wait(barrier, NDP + 1)
    pltpu.make_async_copy(e_v.at[pl.ds(0, 4)], e_v.at[pl.ds(z * 4, 4)], enc_sem).wait()

    def z_copy(direction, step, part):
        back = step - 1
        zc = (z + NZ - back) % NZ if direction == 0 else (z + back) % NZ
        at = zc * 4 + part
        return pltpu.make_async_remote_copy(
            src_ref=e_v.at[at],
            dst_ref=e_v.at[at],
            send_sem=z_send.at[direction, step - 1, part],
            recv_sem=z_recv.at[direction, step - 1, part],
            device_id=ring[direction],
            device_id_type=MESH,
        )

    def near(direction, part):
        return (part < 2) == (direction == 0)

    travel = ((0, 0), (1, 3), (0, 1), (1, 2), (0, 2), (1, 1), (0, 3), (1, 0))
    for direction, part in travel:
        z_copy(direction, 1, part).start()

    def to_line(src, dst, device, here):
        @pl.when(here)
        def _():
            pltpu.make_async_copy(src, dst, el_recv).start()

        @pl.when(jnp.logical_not(here))
        def _():
            pltpu.make_async_remote_copy(
                src_ref=src, dst_ref=dst, send_sem=el_send, recv_sem=el_recv,
                device_id=device, device_id_type=MESH,
            ).start()

    acc[...] = jnp.zeros_like(acc)

    def process(zc):
        blocks = [e_v[zc * 4 + b] for b in range(4)]
        rows = jnp.concatenate(blocks, axis=1)
        w_copy(zc, 0).wait()
        w_copy(zc, 1).wait()
        acc[:, :W2] += mm(rows, kw_v[zc])
        acc[:, W2:] += mm(rows, vw_v[zc])
        for b in range(4):
            et_v[zc * 4 + b] = blocks[b].T
        xc = zc // 2
        half = zc % 2
        to_line(
            et_v.at[pl.ds(zc * 4, 4)], el.at[x * 2 + c, pl.ds(half * 4, 4)],
            (xc * 8 + y * 2, z), (xc == x) & (c == 0),
        )
        for j in range(2):
            yc = half * 2 + j
            to_line(
                et_v.at[pl.ds(zc * 4 + 2 * j, 2)], el.at[y * 2 + c, pl.ds(xc * 2, 2)],
                (x * 8 + yc * 2 + 1, z), (yc == y) & (c == 1),
            )

    process(z)

    def gather_step(k, carry):
        for direction, part in travel:
            z_copy(direction, k, part).wait_recv()
            if near(direction, part):
                z_copy(direction, k + 1, part).start()
            else:
                pl.when(k < 3)(z_copy(direction, k + 1, part).start)
        process((z + NZ - k) % NZ)
        process((z + k) % NZ)
        return carry

    lax.fori_loop(1, 4, gather_step, 0)
    for direction, part in travel[:4]:
        z_copy(direction, 4, part).wait_recv()
    process((z + 4) % NZ)

    def exchange(src, dst, send_sem, recv_sem, h):
        mine = pl.ds(pl.multiple_of(d * SLOT, SLOT), SLOT)
        pltpu.make_async_copy(src.at[h, mine], dst.at[h, mine], recv_sem.at[h]).start()

        def send(i, carry):
            o = (i * 11) % NDP
            t = ((x + o // 8) % 4) * 8 + ((y + (o // 2) % 4) % 4) * 2 + (c + o % 2) % 2
            pltpu.make_async_remote_copy(
                src_ref=src.at[h, pl.ds(pl.multiple_of(t * SLOT, SLOT), SLOT)],
                dst_ref=dst.at[h, mine],
                send_sem=send_sem.at[h],
                recv_sem=recv_sem.at[h],
                device_id=(t, z),
                device_id_type=MESH,
            ).start()
            return carry

        lax.fori_loop(1, NDP, send, 0)

    def drained(buf, sem):
        pltpu.make_async_copy(buf, buf, sem).wait()

    most = pl.ds(0, (NDP - 1) * SLOT)
    hot_b = oh_v[...]
    dead = jnp.sum(hot_b.astype(F32), axis=1, keepdims=True) < 0.5
    for h in range(2):
        cols = pl.ds(h * HD, HD)
        keys = mm(hot_b, acc[:, cols].astype(BF))
        slots[h, :, :HD] = jnp.where(dead, DEAD, keys).astype(BF)
        slots[h, :, HD:] = mm(hot_b, acc[:, pl.ds(W2 + h * HD, HD)].astype(BF)).astype(BF)
        exchange(slots, kvr, kv_send, kv_recv, h)

    n_keys = NDP * SLOT
    dec_col, dec_before = column_of(dec_len[...].astype(F32), NDP)
    same = iota((NDP, n_keys), 1) // SLOT == iota((NDP, n_keys), 0)
    first = jnp.sum(jnp.where(same, dec_before, 0.0), axis=0, keepdims=True)
    last = jnp.sum(jnp.where(same, dec_before + dec_col, 0.0), axis=0, keepdims=True)
    row = iota((DEC, n_keys), 0).astype(F32)
    own = (row >= first) & (row < last)
    q_copy.wait()
    og_copy.wait()
    for h in range(2):
        cols = pl.ds(h * HD, HD)
        drained(kvr.at[h], kv_recv.at[h])
        q = q_v[:, cols]
        g = og_v[:, cols]
        k = kvr[h, :, :HD]
        v = kvr[h, :, HD:]
        total = mm_nt(jnp.ones((16, HD), BF), k)[:1]
        allowed = own & (total < 4.0e6)
        s = jnp.where(allowed, mm_nt(q, k) * (HD ** -0.5), -1e30)
        top = jnp.max(s, axis=1, keepdims=True)
        expo = jnp.exp(s - top)
        probs = expo * (1.0 / jnp.sum(expo, axis=1, keepdims=True))
        weights = probs.astype(BF)
        dw = mm_nt(g, v)
        delta = jnp.sum(probs * dw, axis=1, keepdims=True)
        ds = (probs * (dw - delta) * (HD ** -0.5)).astype(BF)
        gs[h, :, :HD] = mm_tn(ds, q).astype(BF)
        gs[h, :, HD:] = mm_tn(weights, g).astype(BF)
        exchange(gs, gr, g_send, g_recv, h)
        att_v[:, cols] = mm(weights, v).astype(BF)
        qg_v[:, cols] = mm(ds, k).astype(BF)
    att_out = pltpu.make_async_copy(att_v, att_hbm, out_sem.at[0])
    qg_out = pltpu.make_async_copy(qg_v, qg_hbm, out_sem.at[1])
    att_out.start()
    qg_out.start()

    def spread(h):
        def one(kv, i):
            if kv == 0:
                t = ((x + i) % 4) * 8 + y * 2
                at = x * 2 + c
            else:
                t = x * 8 + ((y + i) % 4) * 2 + 1
                at = y * 2 + c
            src = gsend.at[h, kv]
            dst = gl.at[h, pl.ds(pl.multiple_of(at * ROWS, ROWS), ROWS)]

            def far():
                pltpu.make_async_remote_copy(
                    src_ref=src, dst_ref=dst, send_sem=gl_send.at[h], recv_sem=gl_recv.at[h],
                    device_id=(t, z), device_id_type=MESH,
                ).start()

            if i > 0:
                far()
            else:
                pl.when(c != kv)(far)

                @pl.when(c == kv)
                def _():
                    pltpu.make_async_copy(src, dst, gl_recv.at[h]).start()

        for i in (2, 1, 3, 0):
            one(0, i)
            one(1, i)

    def unpack(h):
        drained(gr.at[h], g_recv.at[h])
        rows = mm_tn(oh_v[...], gr[h]).astype(BF)
        gsend[h, 0] = rows[:, :HD]
        gsend[h, 1] = rows[:, HD:]
        spread(h)

    def back(h, zc):
        cols = pl.ds(h * HD, HD)
        return mm_nt(gsend[h, 0], kw_v[zc, :, cols]) + mm_nt(gsend[h, 1], vw_v[zc, :, cols])

    def partial_blocks(h):
        drained(gl.at[h], gl_recv.at[h])

        def block(b, carry):
            lhs = jnp.concatenate([el[j, b] for j in range(8)], axis=1)
            ps[h, b] = mm(lhs, gl[h]).astype(BF)
            t = jnp.where(c == 0, x * 8 + b, (b // 2) * 8 + y * 2 + b % 2)
            dst = cr.at[h, c, jnp.where(c == 0, y, x)]

            @pl.when(t == d)
            def _():
                pltpu.make_async_copy(ps.at[h, b], dst, c_recv.at[h]).start()

            @pl.when(t != d)
            def _():
                pltpu.make_async_remote_copy(
                    src_ref=ps.at[h, b], dst_ref=dst, send_sem=c_send.at[h], recv_sem=c_recv.at[h],
                    device_id=(t, z), device_id_type=MESH,
                ).start()

            return carry

        lax.fori_loop(0, 8, block, 0)

    unpack(0)

    def back_first(zc, carry):
        dx[zc] = back(0, zc)
        return carry

    lax.fori_loop(0, NZ, back_first, 0)
    unpack(1)

    def rs_copy(direction, step, part):
        return pltpu.make_async_remote_copy(
            src_ref=rs_s.at[direction, step - 1, part],
            dst_ref=rs_r.at[direction, step - 1, part],
            send_sem=rs_send.at[direction, step - 1, part],
            recv_sem=rs_recv.at[direction, step - 1, part],
            device_id=ring[direction],
            device_id_type=MESH,
        )

    def rs_part(step, direction, part):
        far = 5 - step
        zc = (z + far) % NZ if direction == 0 else (z + NZ - far) % NZ
        term = dx[zc, :, pl.ds(part * 128, 128)]
        if step >= 3 or (step == 2 and near(direction, part)):
            rs_copy(direction, step - 1, part).wait_recv()
            term = term + rs_r[direction, step - 2, part].astype(F32)
        rs_s[direction, step - 1, part] = term.astype(BF)
        rs_copy(direction, step, part).start()

    def back_second(n, carry):
        zc = chunk_at(7 - n)
        dx[zc] += back(1, zc)
        return carry

    first_parts, last_parts = travel[:4], travel[4:]
    lax.fori_loop(0, 1, back_second, 0)
    for direction, part in first_parts:
        rs_part(1, direction, part)
    lax.fori_loop(1, 3, back_second, 0)
    for direction, part in last_parts:
        rs_part(2, direction, part)
    lax.fori_loop(3, NZ, back_second, 0)
    drained(el, el_recv)
    partial_blocks(0)
    for direction, part in first_parts:
        rs_part(2, direction, part)
    partial_blocks(1)
    for step in (3, 4):
        for direction, part in last_parts + first_parts:
            rs_part(step, direction, part)

    for h in range(2):
        drained(cr.at[h], c_recv.at[h])
        cols = pl.ds(h * HD, HD)
        for kv in range(2):
            total = cr[h, kv, 0].astype(F32)
            for j in range(1, 4):
                total = total + cr[h, kv, j].astype(F32)
            wg_v[kv, :, cols] = total
    kwg_out = pltpu.make_async_copy(wg_v.at[0], kwg_hbm, out_sem.at[2])
    vwg_out = pltpu.make_async_copy(wg_v.at[1], vwg_hbm, out_sem.at[3])
    kwg_out.start()
    vwg_out.start()
    for part in (2, 1, 3, 0):
        cols = pl.ds(part * 128, 128)
        total = dx[z, :, cols]
        for direction in range(2):
            rs_copy(direction, 4, part).wait_recv()
            total = total + rs_r[direction, 3, part].astype(F32)
        eg_v[:, cols] = total.astype(BF)
    eg_out = pltpu.make_async_copy(eg_v, eg_hbm, out_sem.at[4])
    eg_out.start()

    for direction in range(2):
        for step in range(1, 5):
            for part in range(4):
                if step < 4 or near(direction, part):
                    z_copy(direction, step, part).wait_send()
                if step > 1 or near(direction, part):
                    rs_copy(direction, step, part).wait_send()
    drained(el.at[pl.ds(0, 7)], el_send)
    for h in range(2):
        drained(kvr.at[h, most], kv_send.at[h])
        drained(gr.at[h, most], g_send.at[h])
        drained(gl.at[h, pl.ds(0, 7 * ROWS)], gl_send.at[h])
        drained(ps.at[h, pl.ds(0, 7)], c_send.at[h])
    att_out.wait()
    qg_out.wait()
    kwg_out.wait()
    vwg_out.wait()
    eg_out.wait()


def hand_over(*refs):
    given, results, held, sems = refs[:5], refs[5:10], refs[10:15], refs[15]
    inward = [pltpu.make_async_copy(given[i], held[i], sems.at[0, i]) for i in range(5)]
    outward = [pltpu.make_async_copy(held[i], results[i], sems.at[1, i]) for i in range(5)]
    for copy in inward:
        copy.start()
    for i in range(5):
        inward[i].wait()
        outward[i].start()
    for copy in outward:
        copy.wait()


def body(queries, enc_rows, key_weight, value_weight, enc_len, dec_len, route, out_grad):
    any_spec = pl.BlockSpec(memory_space=pl.ANY)
    small = pl.BlockSpec(memory_space=pltpu.VMEM)
    dma = pltpu.SemaphoreType.DMA
    results = (
        jax.ShapeDtypeStruct((DEC, W2), BF),
        jax.ShapeDtypeStruct((DEC, W2), BF),
        jax.ShapeDtypeStruct((ROWS, W2), BF),
        jax.ShapeDtypeStruct((ROWS, W2), F32),
        jax.ShapeDtypeStruct((ROWS, W2), F32),
    )
    made = pl.pallas_call(
        kernel,
        out_shape=results,
        in_specs=[any_spec] * 4 + [small] * 3 + [any_spec],
        out_specs=[any_spec] * 5,
        scratch_shapes=[
            pltpu.VMEM((32, 128, 128), BF),
            pltpu.VMEM((32, 128, 128), BF),
            pltpu.VMEM((NZ, W2, W2), BF),
            pltpu.VMEM((NZ, W2, W2), BF),
            pltpu.VMEM((DEC, W2), BF),
            pltpu.VMEM((DEC, W2), BF),
            pltpu.VMEM((ROWS, 2 * W2), F32),
            pltpu.VMEM((NDP * SLOT, ROWS), BF),
            pltpu.VMEM((2, NDP * SLOT, W2), BF),
            pltpu.VMEM((2, NDP * SLOT, W2), BF),
            pltpu.VMEM((2, NDP * SLOT, W2), BF),
            pltpu.VMEM((2, NDP * SLOT, W2), BF),
            pltpu.VMEM((2, 2, ROWS, HD), BF),
            pltpu.VMEM((2, 8 * ROWS, HD), BF),
            pltpu.VMEM((8, 8, 128, 128), BF),
            pltpu.VMEM((2, 8, 128, HD), BF),
            pltpu.VMEM((2, 2, 4, 128, HD), BF),
            pltpu.VMEM((NZ, ROWS, W2), F32),
            pltpu.VMEM((2, 4, 4, ROWS, 128), BF),
            pltpu.VMEM((2, 4, 4, ROWS, 128), BF),
            pltpu.VMEM((DEC, W2), BF),
            pltpu.VMEM((DEC, W2), BF),
            pltpu.VMEM((ROWS, W2), BF),
            pltpu.VMEM((2, ROWS, W2), F32),
            dma(()),
            dma((NZ, 2)),
            dma((2,)),
            dma((2, 4, 4)),
            dma((2, 4, 4)),
            dma(()),
            dma(()),
            dma((2,)),
            dma((2,)),
            dma((2,)),
            dma((2,)),
            dma((2,)),
            dma((2,)),
            dma((2,)),
            dma((2,)),
            dma((2, 4, 4)),
            dma((2, 4, 4)),
            dma((5,)),
        ],
        compiler_params=pltpu.CompilerParams(
            collective_id=0, has_side_effects=True, vmem_limit_bytes=60 * 1024 * 1024
        ),
    )(queries, enc_rows, key_weight, value_weight, enc_len, dec_len, route, out_grad)
    return pl.pallas_call(
        hand_over,
        out_shape=results,
        in_specs=[any_spec] * 5,
        out_specs=[any_spec] * 5,
        scratch_shapes=[pltpu.VMEM(r.shape, r.dtype) for r in results] + [dma((2, 5))],
        compiler_params=pltpu.CompilerParams(vmem_limit_bytes=60 * 1024 * 1024),
    )(*made)


def solution(mesh):
    in_specs = (
        P("dp", "mp"),
        P("dp", "mp"),
        P(None, "mp"),
        P(None, "mp"),
        P("dp", None),
        P("dp", None),
        P("dp", None),
        P("dp", "mp"),
    )
    out_specs = (P("dp", "mp"), P("dp", "mp"), P("dp", "mp"), P("dp", "mp"), P("dp", "mp"))
    return jax.shard_map(body, mesh=mesh, in_specs=in_specs, out_specs=out_specs, check_vma=False)
```

```python
import jax
import jax.numpy as jnp
from jax import lax
from jax.experimental import pallas as pl
from jax.experimental.pallas import tpu as pltpu
from jax.sharding import PartitionSpec as P

HD = 256
ROWS = 128
DEC = 256
SLOT = 16
NDP = 32
NZ = 8
W2 = 512
FAR = 3
DEAD = 65536.0
MESH = pl.DeviceIdType.MESH
BF = jnp.bfloat16
F32 = jnp.float32


def mm(a, b):
    return lax.dot_general(a, b, (((1,), (0,)), ((), ())), preferred_element_type=F32)


def mm_nt(a, b):
    return lax.dot_general(a, b, (((1,), (1,)), ((), ())), preferred_element_type=F32)


def mm_tn(a, b):
    return lax.dot_general(a, b, (((0,), (0,)), ((), ())), preferred_element_type=F32)


def iota(shape, dim):
    return lax.broadcasted_iota(jnp.int32, shape, dim)


def column_of(row, n):
    here = iota((n, n), 1)
    there = iota((n, n), 0)
    wide = jnp.broadcast_to(row, (n, n))
    col = jnp.sum(jnp.where(here == there, wide, 0.0), axis=1, keepdims=True)
    before = jnp.sum(jnp.where(here < there, wide, 0.0), axis=1, keepdims=True)
    return col, before


def kernel(
    q_hbm, enc_hbm, kw_hbm, vw_hbm, enc_len_hbm, dec_len_hbm, route_hbm, og_hbm,
    att_hbm, qg_hbm, eg_hbm, kwg_hbm, vwg_hbm,
    e_v, et_v, kw_v, vw_v, q_v, og_v, acc, oh_v,
    slots, kvr, gs, gr, gsend, gl, el, ps, cr, dx, rs_s, rs_r,
    att_v, qg_v, eg_v, wg_v, enc_len, dec_len, route,
    enc_sem, w_sem, q_sem, z_send, z_recv, el_send, el_recv, elz_send,
    kv_send, kv_recv, g_send, g_recv, gl_send, gl_recv, c_send, c_recv,
    rs_send, rs_recv, out_sem, int_sem,
):
    d = lax.axis_index("dp")
    z = lax.axis_index("mp")
    x = d // 8
    y = (d // 2) % 4
    c = d % 2
    right = (d, (z + 1) % NZ)
    left = (d, (z + NZ - 1) % NZ)
    ring = (right, left)

    def chunk_at(n):
        off = jnp.where(n % 2 == 1, NZ - (n + 1) // 2, n // 2)
        return (z + off) % NZ

    def drained(buf, sem):
        pltpu.make_async_copy(buf, buf, sem).wait()

    for b in range(4):
        pltpu.make_async_copy(
            enc_hbm.at[:, pl.ds(b * 128, 128)], e_v.at[z * 4 + b], enc_sem
        ).start()

    barrier = pltpu.get_barrier_semaphore()
    for peer in ring:
        pl.semaphore_signal(barrier, inc=1, device_id=peer, device_id_type=MESH)

    def greet(i, carry):
        pl.semaphore_signal(barrier, inc=1, device_id=((d + i) % NDP, z), device_id_type=MESH)
        return carry

    lax.fori_loop(1, NDP, greet, 0)

    def w_copy(zc, kv):
        src, dst = ((kw_hbm, kw_v), (vw_hbm, vw_v))[kv]
        return pltpu.make_async_copy(
            src.at[pl.ds(pl.multiple_of(zc * W2, W2), W2), :], dst.at[zc], w_sem.at[zc, kv]
        )

    def load_w(n, carry):
        zc = chunk_at(n)
        w_copy(zc, 0).start()
        w_copy(zc, 1).start()
        return carry

    lax.fori_loop(0, NZ, load_w, 0)
    q_copy = pltpu.make_async_copy(q_hbm, q_v, q_sem.at[0])
    og_copy = pltpu.make_async_copy(og_hbm, og_v, q_sem.at[1])
    q_copy.start()
    og_copy.start()
    int_copies = [
        pltpu.make_async_copy(src, dst, int_sem.at[i])
        for i, (src, dst) in enumerate(
            ((enc_len_hbm, enc_len), (route_hbm, route), (dec_len_hbm, dec_len))
        )
    ]
    for copy in int_copies:
        copy.start()

    pl.semaphore_wait(barrier, NDP + 1)
    pltpu.make_async_copy(e_v.at[pl.ds(0, 4)], e_v.at[pl.ds(z * 4, 4)], enc_sem).wait()

    def z_copy(direction, step, part):
        back = step - 1
        zc = (z + NZ - back) % NZ if direction == 0 else (z + back) % NZ
        at = zc * 4 + part
        return pltpu.make_async_remote_copy(
            src_ref=e_v.at[at],
            dst_ref=e_v.at[at],
            send_sem=z_send.at[direction, step - 1, part],
            recv_sem=z_recv.at[direction, step - 1, part],
            device_id=ring[direction],
            device_id_type=MESH,
        )

    def near(direction, part):
        return (part < 2) == (direction == 0)

    travel = ((0, 0), (1, 3), (0, 1), (1, 2), (0, 2), (1, 1), (0, 3), (1, 0))
    for direction, part in travel:
        z_copy(direction, 1, part).start()

    def to_line(zc, src, dst, device, here):
        @pl.when(here)
        def _():
            pltpu.make_async_copy(src, dst, el_recv.at[zc]).start()

        @pl.when(jnp.logical_not(here))
        def _():
            pltpu.make_async_remote_copy(
                src_ref=src, dst_ref=dst, send_sem=el_send.at[zc], recv_sem=el_recv.at[zc],
                device_id=device, device_id_type=MESH,
            ).start()

    int_copies[0].wait()
    int_copies[1].wait()
    lens_col, starts_col = column_of(enc_len[...].astype(F32), NDP)
    route_col, _ = column_of(route[...].astype(F32), NDP)
    pos = iota((NDP, ROWS), 1).astype(F32)
    inside = (pos >= starts_col) & (pos < starts_col + lens_col)
    dest = jnp.sum(
        jnp.where(inside, route_col * SLOT + pos - starts_col, 0.0), axis=0, keepdims=True
    )
    hot = iota((NDP * SLOT, ROWS), 0).astype(F32) == dest
    hot_f = jnp.where(hot, 1.0, 0.0)
    oh_v[...] = hot_f.astype(BF)

    acc[...] = jnp.zeros_like(acc)

    def process(zc):
        blocks = [e_v[zc * 4 + b] for b in range(4)]
        rows = jnp.concatenate(blocks, axis=1)
        w_copy(zc, 0).wait()
        w_copy(zc, 1).wait()
        acc[:, :W2] += mm(rows, kw_v[zc])
        acc[:, W2:] += mm(rows, vw_v[zc])
        for b in range(4):
            et_v[zc * 4 + b] = blocks[b].T

    def distribute(zc):
        xc = zc // 2
        half = zc % 2
        to_line(
            zc, et_v.at[pl.ds(zc * 4, 4)], el.at[x * 2 + c, pl.ds(half * 4, 4)],
            (xc * 8 + y * 2, z), (xc == x) & (c == 0),
        )
        for j in range(2):
            yc = half * 2 + j
            to_line(
                zc, et_v.at[pl.ds(zc * 4 + 2 * j, 2)], el.at[y * 2 + c, pl.ds(xc * 2, 2)],
                (x * 8 + yc * 2 + 1, z), (yc == y) & (c == 1),
            )

    process(z)
    distribute(z)

    def gather_step(k, carry):
        for direction, part in travel:
            z_copy(direction, k, part).wait_recv()
            if near(direction, part):
                z_copy(direction, k + 1, part).start()
            else:
                pl.when(k < 3)(z_copy(direction, k + 1, part).start)
        for zc in ((z + NZ - k) % NZ, (z + k) % NZ):
            process(zc)
            pl.when(k < FAR)(lambda: distribute(zc))
        return carry

    lax.fori_loop(1, 4, gather_step, 0)
    for direction, part in travel[:4]:
        z_copy(direction, 4, part).wait_recv()
    process((z + 4) % NZ)

    def line_blocks(zc, core):
        return pl.ds((zc % 2) * 4, 4) if core == 0 else pl.ds((zc // 2) * 2, 2)

    def on_holder(zc, fn):
        pl.when((c == 0) & (zc // 2 == x))(lambda: fn(0))
        pl.when((c == 1) & (zc % 2 == y // 2))(lambda: fn(1))

    def wait_line(zc):
        def one(core):
            drained(el.at[:, line_blocks(zc, core)], el_recv.at[zc])

        on_holder(zc, one)

    def along_z(n, act):
        zc, step, first, count = (
            (z + 2, 7, 0, 8), (z + 6, 1, 0, 8),
        )[n]
        zc = zc % NZ

        def one(core):
            at = el.at[pl.ds(first, count), line_blocks(zc, core)]
            act(pltpu.make_async_remote_copy(
                src_ref=at, dst_ref=at, send_sem=elz_send.at[n], recv_sem=el_recv.at[zc],
                device_id=(d, (z + step) % NZ), device_id_type=MESH,
            ))

        on_holder(zc, one)

    def exchange(src, dst, send_sem, recv_sem, h):
        mine = pl.ds(pl.multiple_of(d * SLOT, SLOT), SLOT)
        pltpu.make_async_copy(src.at[h, mine], dst.at[h, mine], recv_sem.at[h]).start()

        def send(i, carry):
            o = (i * 11) % NDP
            t = ((x + o // 8) % 4) * 8 + ((y + (o // 2) % 4) % 4) * 2 + (c + o % 2) % 2
            pltpu.make_async_remote_copy(
                src_ref=src.at[h, pl.ds(pl.multiple_of(t * SLOT, SLOT), SLOT)],
                dst_ref=dst.at[h, mine],
                send_sem=send_sem.at[h],
                recv_sem=recv_sem.at[h],
                device_id=(t, z),
                device_id_type=MESH,
            ).start()
            return carry

        lax.fori_loop(1, NDP, send, 0)

    most = pl.ds(0, (NDP - 1) * SLOT)
    hot_b = oh_v[...]
    dead = jnp.sum(hot_b.astype(F32), axis=1, keepdims=True) < 0.5
    for h in range(2):
        cols = pl.ds(h * HD, HD)
        keys = mm(hot_b, acc[:, cols].astype(BF))
        slots[h, :, :HD] = jnp.where(dead, DEAD, keys).astype(BF)
        slots[h, :, HD:] = mm(hot_b, acc[:, pl.ds(W2 + h * HD, HD)].astype(BF)).astype(BF)
        exchange(slots, kvr, kv_send, kv_recv, h)
    distribute((z + 4) % NZ)

    for k in (2, 6):
        wait_line((z + k) % NZ)
    for n in range(2):
        along_z(n, lambda copy: copy.start())

    n_keys = NDP * SLOT
    int_copies[2].wait()
    dec_col, dec_before = column_of(dec_len[...].astype(F32), NDP)
    same = iota((NDP, n_keys), 1) // SLOT == iota((NDP, n_keys), 0)
    first = jnp.sum(jnp.where(same, dec_before, 0.0), axis=0, keepdims=True)
    last = jnp.sum(jnp.where(same, dec_before + dec_col, 0.0), axis=0, keepdims=True)
    row = iota((DEC, n_keys), 0).astype(F32)
    own = (row >= first) & (row < last)
    q_copy.wait()
    og_copy.wait()
    for h in range(2):
        cols = pl.ds(h * HD, HD)
        drained(kvr.at[h], kv_recv.at[h])
        q = q_v[:, cols]
        g = og_v[:, cols]
        k = kvr[h, :, :HD]
        v = kvr[h, :, HD:]
        total = mm_nt(jnp.ones((16, HD), BF), k)[:1]
        allowed = own & (total < 4.0e6)
        s = jnp.where(allowed, mm_nt(q, k) * (HD ** -0.5), -1e30)
        top = jnp.max(s, axis=1, keepdims=True)
        expo = jnp.exp(s - top)
        probs = expo * (1.0 / jnp.sum(expo, axis=1, keepdims=True))
        weights = probs.astype(BF)
        dw = mm_nt(g, v)
        delta = jnp.sum(probs * dw, axis=1, keepdims=True)
        ds = (probs * (dw - delta) * (HD ** -0.5)).astype(BF)
        gs[h, :, :HD] = mm_tn(ds, q).astype(BF)
        gs[h, :, HD:] = mm_tn(weights, g).astype(BF)
        exchange(gs, gr, g_send, g_recv, h)
        att_v[:, cols] = mm(weights, v).astype(BF)
        qg_v[:, cols] = mm(ds, k).astype(BF)
    att_out = pltpu.make_async_copy(att_v, att_hbm, out_sem.at[0])
    qg_out = pltpu.make_async_copy(qg_v, qg_hbm, out_sem.at[1])
    att_out.start()
    qg_out.start()

    def spread(h):
        def one(kv, i):
            if kv == 0:
                t = ((x + i) % 4) * 8 + y * 2
                at = x * 2 + c
            else:
                t = x * 8 + ((y + i) % 4) * 2 + 1
                at = y * 2 + c
            src = gsend.at[h, kv]
            dst = gl.at[h, pl.ds(pl.multiple_of(at * ROWS, ROWS), ROWS)]

            def far():
                pltpu.make_async_remote_copy(
                    src_ref=src, dst_ref=dst, send_sem=gl_send.at[h], recv_sem=gl_recv.at[h],
                    device_id=(t, z), device_id_type=MESH,
                ).start()

            if i > 0:
                far()
            else:
                pl.when(c != kv)(far)

                @pl.when(c == kv)
                def _():
                    pltpu.make_async_copy(src, dst, gl_recv.at[h]).start()

        for i in (2, 1, 3, 0):
            one(0, i)
            one(1, i)

    def unpack(h):
        drained(gr.at[h], g_recv.at[h])
        rows = mm_tn(oh_v[...], gr[h]).astype(BF)
        gsend[h, 0] = rows[:, :HD]
        gsend[h, 1] = rows[:, HD:]
        spread(h)

    def back(h, zc):
        cols = pl.ds(h * HD, HD)
        return mm_nt(gsend[h, 0], kw_v[zc, :, cols]) + mm_nt(gsend[h, 1], vw_v[zc, :, cols])

    def partial_blocks(h):
        drained(gl.at[h], gl_recv.at[h])

        def block(b, carry):
            lhs = jnp.concatenate([el[j, b] for j in range(8)], axis=1)
            ps[h, b] = mm(lhs, gl[h]).astype(BF)
            t = jnp.where(c == 0, x * 8 + b, (b // 2) * 8 + y * 2 + b % 2)
            dst = cr.at[h, c, jnp.where(c == 0, y, x)]

            @pl.when(t == d)
            def _():
                pltpu.make_async_copy(ps.at[h, b], dst, c_recv.at[h]).start()

            @pl.when(t != d)
            def _():
                pltpu.make_async_remote_copy(
                    src_ref=ps.at[h, b], dst_ref=dst, send_sem=c_send.at[h], recv_sem=c_recv.at[h],
                    device_id=(t, z), device_id_type=MESH,
                ).start()

            return carry

        lax.fori_loop(0, 8, block, 0)

    unpack(0)

    def back_first(zc, carry):
        dx[zc] = back(0, zc)
        return carry

    lax.fori_loop(0, NZ, back_first, 0)
    unpack(1)

    def rs_copy(direction, step, part):
        return pltpu.make_async_remote_copy(
            src_ref=rs_s.at[direction, step - 1, part],
            dst_ref=rs_r.at[direction, step - 1, part],
            send_sem=rs_send.at[direction, step - 1, part],
            recv_sem=rs_recv.at[direction, step - 1, part],
            device_id=ring[direction],
            device_id_type=MESH,
        )

    def rs_part(step, direction, part):
        far = 5 - step
        zc = (z + far) % NZ if direction == 0 else (z + NZ - far) % NZ
        term = dx[zc, :, pl.ds(part * 128, 128)]
        if step >= 3 or (step == 2 and near(direction, part)):
            rs_copy(direction, step - 1, part).wait_recv()
            term = term + rs_r[direction, step - 2, part].astype(F32)
        rs_s[direction, step - 1, part] = term.astype(BF)
        rs_copy(direction, step, part).start()

    def back_second(n, carry):
        zc = chunk_at(7 - n)
        dx[zc] += back(1, zc)
        return carry

    first_parts, last_parts = travel[:4], travel[4:]
    lax.fori_loop(0, 1, back_second, 0)
    for direction, part in first_parts:
        rs_part(1, direction, part)
    lax.fori_loop(1, 3, back_second, 0)
    for direction, part in last_parts:
        rs_part(2, direction, part)
    lax.fori_loop(3, NZ, back_second, 0)
    for k in (0, 1, 7, 3, 5, 4):
        wait_line((z + k) % NZ)
    partial_blocks(0)
    for direction, part in first_parts:
        rs_part(2, direction, part)
    partial_blocks(1)
    for step in (3, 4):
        for direction, part in last_parts + first_parts:
            rs_part(step, direction, part)

    for h in range(2):
        drained(cr.at[h], c_recv.at[h])
        cols = pl.ds(h * HD, HD)
        for kv in range(2):
            total = cr[h, kv, 0].astype(F32)
            for j in range(1, 4):
                total = total + cr[h, kv, j].astype(F32)
            wg_v[kv, :, cols] = total
    kwg_out = pltpu.make_async_copy(wg_v.at[0], kwg_hbm, out_sem.at[2])
    vwg_out = pltpu.make_async_copy(wg_v.at[1], vwg_hbm, out_sem.at[3])
    kwg_out.start()
    vwg_out.start()
    for part in (2, 1, 3, 0):
        cols = pl.ds(part * 128, 128)
        total = dx[z, :, cols]
        for direction in range(2):
            rs_copy(direction, 4, part).wait_recv()
            total = total + rs_r[direction, 3, part].astype(F32)
        eg_v[:, cols] = total.astype(BF)
    eg_out = pltpu.make_async_copy(eg_v, eg_hbm, out_sem.at[4])
    eg_out.start()

    for direction in range(2):
        for step in range(1, 5):
            for part in range(4):
                if step < 4 or near(direction, part):
                    z_copy(direction, step, part).wait_send()
                if step > 1 or near(direction, part):
                    rs_copy(direction, step, part).wait_send()
    for k in (0, 1, 7, 2, 6, 4):
        zc = (z + k) % NZ
        own_x = (c == 0) & (zc // 2 == x)
        own_y = (c == 1) & (zc % 2 == y // 2)
        pl.when(own_x)(lambda: drained(et_v.at[pl.ds(0, 4)], el_send.at[zc]))
        pl.when(own_y)(lambda: drained(et_v.at[pl.ds(0, 6)], el_send.at[zc]))
        other = jnp.logical_not(own_x | own_y)
        pl.when(other)(lambda: drained(et_v.at[pl.ds(0, 8)], el_send.at[zc]))
    for n in range(2):
        along_z(n, lambda copy: copy.wait_send())
    for h in range(2):
        drained(kvr.at[h, most], kv_send.at[h])
        drained(gr.at[h, most], g_send.at[h])
        drained(gl.at[h, pl.ds(0, 7 * ROWS)], gl_send.at[h])
        drained(ps.at[h, pl.ds(0, 7)], c_send.at[h])
    att_out.wait()
    qg_out.wait()
    kwg_out.wait()
    vwg_out.wait()
    eg_out.wait()


def hand_over(*refs):
    given, results, held, sems = refs[:5], refs[5:10], refs[10:15], refs[15]
    inward = [pltpu.make_async_copy(given[i], held[i], sems.at[0, i]) for i in range(5)]
    outward = [pltpu.make_async_copy(held[i], results[i], sems.at[1, i]) for i in range(5)]
    for copy in inward:
        copy.start()
    for i in range(5):
        inward[i].wait()
        outward[i].start()
    for copy in outward:
        copy.wait()


def body(queries, enc_rows, key_weight, value_weight, enc_len, dec_len, route, out_grad):
    any_spec = pl.BlockSpec(memory_space=pl.ANY)
    dma = pltpu.SemaphoreType.DMA
    results = (
        jax.ShapeDtypeStruct((DEC, W2), BF),
        jax.ShapeDtypeStruct((DEC, W2), BF),
        jax.ShapeDtypeStruct((ROWS, W2), BF),
        jax.ShapeDtypeStruct((ROWS, W2), F32),
        jax.ShapeDtypeStruct((ROWS, W2), F32),
    )
    made = pl.pallas_call(
        kernel,
        out_shape=results,
        in_specs=[any_spec] * 8,
        out_specs=[any_spec] * 5,
        scratch_shapes=[
            pltpu.VMEM((32, 128, 128), BF),
            pltpu.VMEM((32, 128, 128), BF),
            pltpu.VMEM((NZ, W2, W2), BF),
            pltpu.VMEM((NZ, W2, W2), BF),
            pltpu.VMEM((DEC, W2), BF),
            pltpu.VMEM((DEC, W2), BF),
            pltpu.VMEM((ROWS, 2 * W2), F32),
            pltpu.VMEM((NDP * SLOT, ROWS), BF),
            pltpu.VMEM((2, NDP * SLOT, W2), BF),
            pltpu.VMEM((2, NDP * SLOT, W2), BF),
            pltpu.VMEM((2, NDP * SLOT, W2), BF),
            pltpu.VMEM((2, NDP * SLOT, W2), BF),
            pltpu.VMEM((2, 2, ROWS, HD), BF),
            pltpu.VMEM((2, 8 * ROWS, HD), BF),
            pltpu.VMEM((8, 8, 128, 128), BF),
            pltpu.VMEM((2, 8, 128, HD), BF),
            pltpu.VMEM((2, 2, 4, 128, HD), BF),
            pltpu.VMEM((NZ, ROWS, W2), F32),
            pltpu.VMEM((2, 4, 4, ROWS, 128), BF),
            pltpu.VMEM((2, 4, 4, ROWS, 128), BF),
            pltpu.VMEM((DEC, W2), BF),
            pltpu.VMEM((DEC, W2), BF),
            pltpu.VMEM((ROWS, W2), BF),
            pltpu.VMEM((2, ROWS, W2), F32),
            pltpu.VMEM((1, NDP), jnp.int32),
            pltpu.VMEM((1, NDP), jnp.int32),
            pltpu.VMEM((1, NDP), jnp.int32),
            dma(()),
            dma((NZ, 2)),
            dma((2,)),
            dma((2, 4, 4)),
            dma((2, 4, 4)),
            dma((NZ,)),
            dma((NZ,)),
            dma((2,)),
            dma((2,)),
            dma((2,)),
            dma((2,)),
            dma((2,)),
            dma((2,)),
            dma((2,)),
            dma((2,)),
            dma((2,)),
            dma((2, 4, 4)),
            dma((2, 4, 4)),
            dma((5,)),
            dma((3,)),
        ],
        compiler_params=pltpu.CompilerParams(
            collective_id=0, has_side_effects=True, vmem_limit_bytes=60 * 1024 * 1024
        ),
    )(queries, enc_rows, key_weight, value_weight, enc_len, dec_len, route, out_grad)
    return pl.pallas_call(
        hand_over,
        out_shape=results,
        in_specs=[any_spec] * 5,
        out_specs=[any_spec] * 5,
        scratch_shapes=[pltpu.VMEM(r.shape, r.dtype) for r in results] + [dma((2, 5))],
        compiler_params=pltpu.CompilerParams(vmem_limit_bytes=60 * 1024 * 1024),
    )(*made)


def solution(mesh):
    in_specs = (
        P("dp", "mp"),
        P("dp", "mp"),
        P(None, "mp"),
        P(None, "mp"),
        P("dp", None),
        P("dp", None),
        P("dp", None),
        P("dp", "mp"),
    )
    out_specs = (P("dp", "mp"), P("dp", "mp"), P("dp", "mp"), P("dp", "mp"), P("dp", "mp"))
    return jax.shard_map(body, mesh=mesh, in_specs=in_specs, out_specs=out_specs, check_vma=False)
```

```python
import jax
import jax.numpy as jnp
from jax import lax
from jax.experimental import pallas as pl
from jax.experimental.pallas import tpu as pltpu
from jax.sharding import PartitionSpec as P

HD = 256
ROWS = 128
DEC = 256
SLOT = 16
NDP = 32
NZ = 8
W2 = 512
FAR = 3
DEAD = 65536.0
FARTHEST_FIRST = (10, 6, 9, 14, 11, 5, 8, 15, 2, 7, 13, 4, 1, 12, 3)
MESH = pl.DeviceIdType.MESH
BF = jnp.bfloat16
F32 = jnp.float32


def mm(a, b):
    return lax.dot_general(a, b, (((1,), (0,)), ((), ())), preferred_element_type=F32)


def mm_nt(a, b):
    return lax.dot_general(a, b, (((1,), (1,)), ((), ())), preferred_element_type=F32)


def mm_tn(a, b):
    return lax.dot_general(a, b, (((0,), (0,)), ((), ())), preferred_element_type=F32)


def iota(shape, dim):
    return lax.broadcasted_iota(jnp.int32, shape, dim)


def column_of(row, n):
    here = iota((n, n), 1)
    there = iota((n, n), 0)
    wide = jnp.broadcast_to(row, (n, n))
    col = jnp.sum(jnp.where(here == there, wide, 0.0), axis=1, keepdims=True)
    before = jnp.sum(jnp.where(here < there, wide, 0.0), axis=1, keepdims=True)
    return col, before


def kernel(
    q_hbm, enc_hbm, kw_hbm, vw_hbm, enc_len_hbm, dec_len_hbm, route_hbm, og_hbm,
    att_hbm, qg_hbm, eg_hbm, kwg_hbm, vwg_hbm,
    e_v, et_v, kw_v, vw_v, q_v, og_v, acc, oh_v, oht_v,
    slots, kvr, gs, gr, gsend, gl, el, ps, cr, dx, rs_s, rs_r,
    att_v, qg_v, eg_v, wg_v, enc_len, dec_len, route,
    enc_sem, w_sem, q_sem, z_send, z_recv, el_send, el_recv, elz_send,
    kv_send, kv_recv, g_send, g_recv, gl_send, gl_recv, c_send, c_recv,
    rs_send, rs_recv, out_sem, int_sem,
):
    d = lax.axis_index("dp")
    z = lax.axis_index("mp")
    x = d // 8
    y = (d // 2) % 4
    c = d % 2
    right = (d, (z + 1) % NZ)
    left = (d, (z + NZ - 1) % NZ)
    ring = (right, left)

    def chunk_at(n):
        off = jnp.where(n % 2 == 1, NZ - (n + 1) // 2, n // 2)
        return (z + off) % NZ

    def drained(buf, sem):
        pltpu.make_async_copy(buf, buf, sem).wait()

    for b in range(4):
        pltpu.make_async_copy(
            enc_hbm.at[:, pl.ds(b * 128, 128)], e_v.at[z * 4 + b], enc_sem
        ).start()

    barrier = pltpu.get_barrier_semaphore()
    for peer in ring:
        pl.semaphore_signal(barrier, inc=1, device_id=peer, device_id_type=MESH)

    def greet(i, carry):
        pl.semaphore_signal(barrier, inc=1, device_id=((d + i) % NDP, z), device_id_type=MESH)
        return carry

    lax.fori_loop(1, NDP, greet, 0)

    def w_copy(zc, kv):
        src, dst = ((kw_hbm, kw_v), (vw_hbm, vw_v))[kv]
        return pltpu.make_async_copy(
            src.at[pl.ds(pl.multiple_of(zc * W2, W2), W2), :], dst.at[zc], w_sem.at[zc, kv]
        )

    def load_w(n, carry):
        zc = chunk_at(n)
        w_copy(zc, 0).start()
        w_copy(zc, 1).start()
        return carry

    int_copies = [
        pltpu.make_async_copy(src, dst, int_sem.at[i])
        for i, (src, dst) in enumerate(
            ((enc_len_hbm, enc_len), (route_hbm, route), (dec_len_hbm, dec_len))
        )
    ]
    for copy in int_copies:
        copy.start()

    pl.semaphore_wait(barrier, NDP + 1)
    pltpu.make_async_copy(e_v.at[pl.ds(0, 4)], e_v.at[pl.ds(z * 4, 4)], enc_sem).wait()

    def z_copy(direction, step, part):
        back = step - 1
        zc = (z + NZ - back) % NZ if direction == 0 else (z + back) % NZ
        at = zc * 4 + part
        return pltpu.make_async_remote_copy(
            src_ref=e_v.at[at],
            dst_ref=e_v.at[at],
            send_sem=z_send.at[direction, step - 1, part],
            recv_sem=z_recv.at[direction, step - 1, part],
            device_id=ring[direction],
            device_id_type=MESH,
        )

    def near(direction, part):
        return (part < 2) == (direction == 0)

    travel = ((0, 0), (1, 3), (0, 1), (1, 2), (0, 2), (1, 1), (0, 3), (1, 0))
    for direction, part in travel:
        z_copy(direction, 1, part).start()
    lax.fori_loop(0, NZ, load_w, 0)
    q_copy = pltpu.make_async_copy(q_hbm, q_v, q_sem.at[0])
    og_copy = pltpu.make_async_copy(og_hbm, og_v, q_sem.at[1])
    q_copy.start()
    og_copy.start()

    def to_line(zc, src, dst, device, here):
        @pl.when(here)
        def _():
            pltpu.make_async_copy(src, dst, el_recv.at[zc]).start()

        @pl.when(jnp.logical_not(here))
        def _():
            pltpu.make_async_remote_copy(
                src_ref=src, dst_ref=dst, send_sem=el_send.at[zc], recv_sem=el_recv.at[zc],
                device_id=device, device_id_type=MESH,
            ).start()

    int_copies[0].wait()
    int_copies[1].wait()
    lens_col, starts_col = column_of(enc_len[...].astype(F32), NDP)
    route_col, _ = column_of(route[...].astype(F32), NDP)
    pos = iota((NDP, ROWS), 1).astype(F32)
    inside = (pos >= starts_col) & (pos < starts_col + lens_col)
    dest = jnp.sum(
        jnp.where(inside, route_col * SLOT + pos - starts_col, 0.0), axis=0, keepdims=True
    )
    hot = iota((NDP * SLOT, ROWS), 0).astype(F32) == dest
    hot_f = jnp.where(hot, 1.0, 0.0)
    oh_v[...] = hot_f.astype(BF)

    acc[...] = jnp.zeros_like(acc)

    def process(zc):
        blocks = [e_v[zc * 4 + b] for b in range(4)]
        rows = jnp.concatenate(blocks, axis=1)
        w_copy(zc, 0).wait()
        w_copy(zc, 1).wait()
        acc[:, :W2] += mm(rows, kw_v[zc])
        acc[:, W2:] += mm(rows, vw_v[zc])
        for b in range(4):
            et_v[zc * 4 + b] = blocks[b].T

    def distribute(zc):
        xc = zc // 2
        half = zc % 2
        to_line(
            zc, et_v.at[pl.ds(zc * 4, 4)], el.at[x * 2 + c, pl.ds(half * 4, 4)],
            (xc * 8 + y * 2, z), (xc == x) & (c == 0),
        )
        for j in range(2):
            yc = half * 2 + j
            to_line(
                zc, et_v.at[pl.ds(zc * 4 + 2 * j, 2)], el.at[y * 2 + c, pl.ds(xc * 2, 2)],
                (x * 8 + yc * 2 + 1, z), (yc == y) & (c == 1),
            )

    process(z)
    distribute(z)

    def gather_step(k, carry):
        for direction, part in travel:
            z_copy(direction, k, part).wait_recv()
            if near(direction, part):
                z_copy(direction, k + 1, part).start()
            else:
                pl.when(k < 3)(z_copy(direction, k + 1, part).start)
        for zc in ((z + NZ - k) % NZ, (z + k) % NZ):
            process(zc)
            pl.when(k < FAR)(lambda: distribute(zc))
        return carry

    lax.fori_loop(1, 4, gather_step, 0)
    for direction, part in travel[:4]:
        z_copy(direction, 4, part).wait_recv()
    process((z + 4) % NZ)

    def line_blocks(zc, core):
        return pl.ds((zc % 2) * 4, 4) if core == 0 else pl.ds((zc // 2) * 2, 2)

    def on_holder(zc, fn):
        pl.when((c == 0) & (zc // 2 == x))(lambda: fn(0))
        pl.when((c == 1) & (zc % 2 == y // 2))(lambda: fn(1))

    def wait_line(zc):
        def one(core):
            drained(el.at[:, line_blocks(zc, core)], el_recv.at[zc])

        on_holder(zc, one)

    def along_z(n, act):
        zc, step, first, count = (
            (z + 2, 7, 0, 8), (z + 6, 1, 0, 8),
        )[n]
        zc = zc % NZ

        def one(core):
            at = el.at[pl.ds(first, count), line_blocks(zc, core)]
            act(pltpu.make_async_remote_copy(
                src_ref=at, dst_ref=at, send_sem=elz_send.at[n], recv_sem=el_recv.at[zc],
                device_id=(d, (z + step) % NZ), device_id_type=MESH,
            ))

        on_holder(zc, one)

    def exchange(src, dst, send_sem, recv_sem, h):
        mine = pl.ds(pl.multiple_of(d * SLOT, SLOT), SLOT)
        pltpu.make_async_copy(src.at[h, mine], dst.at[h, mine], recv_sem.at[h]).start()

        def send(i, carry):
            o = jnp.int32(0)
            for n in range(15):
                o = jnp.where(i // 2 == n, FARTHEST_FIRST[n], o)
            t = ((x + o // 4) % 4) * 8 + ((y + o % 4) % 4) * 2 + (c + i + 1) % 2
            pltpu.make_async_remote_copy(
                src_ref=src.at[h, pl.ds(pl.multiple_of(t * SLOT, SLOT), SLOT)],
                dst_ref=dst.at[h, mine],
                send_sem=send_sem.at[h],
                recv_sem=recv_sem.at[h],
                device_id=(t, z),
                device_id_type=MESH,
            ).start()
            return carry

        lax.fori_loop(0, NDP - 1, send, 0)

    most = pl.ds(0, (NDP - 1) * SLOT)
    hot_b = oh_v[...]
    dead = jnp.sum(hot_b.astype(F32), axis=1, keepdims=True) < 0.5
    for h in range(2):
        cols = pl.ds(h * HD, HD)
        keys = mm(hot_b, acc[:, cols].astype(BF))
        slots[h, :, :HD] = jnp.where(dead, DEAD, keys).astype(BF)
        slots[h, :, HD:] = mm(hot_b, acc[:, pl.ds(W2 + h * HD, HD)].astype(BF)).astype(BF)
        exchange(slots, kvr, kv_send, kv_recv, h)
    distribute((z + 4) % NZ)

    def relay():
        for k in (2, 6):
            wait_line((z + k) % NZ)
        for n in range(2):
            along_z(n, lambda copy: copy.start())


    oht_v[...] = hot_b.T

    n_keys = NDP * SLOT
    int_copies[2].wait()
    dec_col, dec_before = column_of(dec_len[...].astype(F32), NDP)
    same = iota((NDP, n_keys), 1) // SLOT == iota((NDP, n_keys), 0)
    first = jnp.sum(jnp.where(same, dec_before, 0.0), axis=0, keepdims=True)
    last = jnp.sum(jnp.where(same, dec_before + dec_col, 0.0), axis=0, keepdims=True)
    row = iota((DEC, n_keys), 0).astype(F32)
    own = (row >= first) & (row < last)
    q_copy.wait()
    og_copy.wait()
    for h in range(2):
        cols = pl.ds(h * HD, HD)
        drained(kvr.at[h], kv_recv.at[h])
        q = q_v[:, cols]
        g = og_v[:, cols]
        k = kvr[h, :, :HD]
        v = kvr[h, :, HD:]
        total = mm_nt(jnp.ones((16, HD), BF), k)[:1]
        allowed = own & (total < 4.0e6)
        s = jnp.where(allowed, mm_nt(q, k) * (HD ** -0.5), -1e30)
        top = jnp.max(s, axis=1, keepdims=True)
        expo = jnp.exp(s - top)
        probs = expo * (1.0 / jnp.sum(expo, axis=1, keepdims=True))
        weights = probs.astype(BF)
        dw = mm_nt(g, v)
        delta = jnp.sum(probs * dw, axis=1, keepdims=True)
        ds = (probs * (dw - delta) * (HD ** -0.5)).astype(BF)
        gs[h, :, :HD] = mm_tn(ds, q).astype(BF)
        gs[h, :, HD:] = mm_tn(weights, g).astype(BF)
        exchange(gs, gr, g_send, g_recv, h)
        if h == 0:
            relay()
        att_v[:, cols] = mm(weights, v).astype(BF)
        qg_v[:, cols] = mm(ds, k).astype(BF)
    att_out = pltpu.make_async_copy(att_v, att_hbm, out_sem.at[0])
    qg_out = pltpu.make_async_copy(qg_v, qg_hbm, out_sem.at[1])
    att_out.start()
    qg_out.start()

    def spread(h):
        def one(kv, i):
            if kv == 0:
                t = ((x + i) % 4) * 8 + y * 2
                at = x * 2 + c
            else:
                t = x * 8 + ((y + i) % 4) * 2 + 1
                at = y * 2 + c
            src = gsend.at[h, kv]
            dst = gl.at[h, pl.ds(pl.multiple_of(at * ROWS, ROWS), ROWS)]

            def far():
                pltpu.make_async_remote_copy(
                    src_ref=src, dst_ref=dst, send_sem=gl_send.at[h], recv_sem=gl_recv.at[h],
                    device_id=(t, z), device_id_type=MESH,
                ).start()

            if i > 0:
                far()
            else:
                pl.when(c != kv)(far)

                @pl.when(c == kv)
                def _():
                    pltpu.make_async_copy(src, dst, gl_recv.at[h]).start()

        for i in (2, 1, 3, 0):
            one(0, i)
            one(1, i)

    def unpack(h):
        drained(gr.at[h], g_recv.at[h])
        rows = mm(oht_v[...], gr[h]).astype(BF)
        gsend[h, 0] = rows[:, :HD]
        gsend[h, 1] = rows[:, HD:]
        spread(h)

    def back(h, zc):
        cols = pl.ds(h * HD, HD)
        return mm_nt(gsend[h, 0], kw_v[zc, :, cols]) + mm_nt(gsend[h, 1], vw_v[zc, :, cols])

    def send_block(h, b):
        t = jnp.where(c == 0, x * 8 + b, (b // 2) * 8 + y * 2 + b % 2)
        dst = cr.at[h, c, jnp.where(c == 0, y, x)]

        @pl.when(t == d)
        def _():
            pltpu.make_async_copy(ps.at[h, b], dst, c_recv.at[h]).start()

        @pl.when(t != d)
        def _():
            pltpu.make_async_remote_copy(
                src_ref=ps.at[h, b], dst_ref=dst, send_sem=c_send.at[h], recv_sem=c_recv.at[h],
                device_id=(t, z), device_id_type=MESH,
            ).start()

    def partial_blocks(h):
        drained(gl.at[h], gl_recv.at[h])

        def blocks(n, carry):
            lhs = jnp.concatenate(
                [
                    jnp.concatenate([el[j, n * 4 + i] for j in range(8)], axis=1)
                    for i in range(4)
                ],
                axis=0,
            )
            out = mm(lhs, gl[h]).astype(BF)
            for i in range(4):
                ps[h, n * 4 + i] = out[i * 128:(i + 1) * 128]
                send_block(h, n * 4 + i)
            return carry

        lax.fori_loop(0, 2, blocks, 0)

    unpack(0)

    def back_first(zc, carry):
        dx[zc] = back(0, zc)
        return carry

    lax.fori_loop(0, NZ, back_first, 0)
    unpack(1)

    def rs_copy(direction, step, part):
        return pltpu.make_async_remote_copy(
            src_ref=rs_s.at[direction, step - 1, part],
            dst_ref=rs_r.at[direction, step - 1, part],
            send_sem=rs_send.at[direction, step - 1, part],
            recv_sem=rs_recv.at[direction, step - 1, part],
            device_id=ring[direction],
            device_id_type=MESH,
        )

    def rs_part(step, direction, part):
        far = 5 - step
        zc = (z + far) % NZ if direction == 0 else (z + NZ - far) % NZ
        term = dx[zc, :, pl.ds(part * 128, 128)]
        if step >= 3 or (step == 2 and near(direction, part)):
            rs_copy(direction, step - 1, part).wait_recv()
            term = term + rs_r[direction, step - 2, part].astype(F32)
        rs_s[direction, step - 1, part] = term.astype(BF)
        rs_copy(direction, step, part).start()

    def back_second(n, carry):
        zc = chunk_at(7 - n)
        dx[zc] += back(1, zc)
        return carry

    first_parts, last_parts = travel[:4], travel[4:]
    lax.fori_loop(0, 1, back_second, 0)
    for direction, part in first_parts:
        rs_part(1, direction, part)
    lax.fori_loop(1, 3, back_second, 0)
    for direction, part in last_parts:
        rs_part(2, direction, part)
    lax.fori_loop(3, NZ, back_second, 0)
    for k in (0, 1, 7, 3, 5, 4):
        wait_line((z + k) % NZ)
    partial_blocks(0)
    for direction, part in first_parts:
        rs_part(2, direction, part)
    partial_blocks(1)
    for step in (3, 4):
        for direction, part in last_parts + first_parts:
            rs_part(step, direction, part)

    for h in range(2):
        drained(cr.at[h], c_recv.at[h])
        cols = pl.ds(h * HD, HD)
        for kv in range(2):
            total = cr[h, kv, 0].astype(F32)
            for j in range(1, 4):
                total = total + cr[h, kv, j].astype(F32)
            wg_v[kv, :, cols] = total
    kwg_out = pltpu.make_async_copy(wg_v.at[0], kwg_hbm, out_sem.at[2])
    vwg_out = pltpu.make_async_copy(wg_v.at[1], vwg_hbm, out_sem.at[3])
    kwg_out.start()
    vwg_out.start()
    for part in (2, 1, 3, 0):
        cols = pl.ds(part * 128, 128)
        total = dx[z, :, cols]
        for direction in range(2):
            rs_copy(direction, 4, part).wait_recv()
            total = total + rs_r[direction, 3, part].astype(F32)
        eg_v[:, cols] = total.astype(BF)
    eg_out = pltpu.make_async_copy(eg_v, eg_hbm, out_sem.at[4])
    eg_out.start()

    for direction in range(2):
        for step in range(1, 5):
            for part in range(4):
                if step < 4 or near(direction, part):
                    z_copy(direction, step, part).wait_send()
                if step > 1 or near(direction, part):
                    rs_copy(direction, step, part).wait_send()
    for k in (0, 1, 7, 2, 6, 4):
        zc = (z + k) % NZ
        own_x = (c == 0) & (zc // 2 == x)
        own_y = (c == 1) & (zc % 2 == y // 2)
        pl.when(own_x)(lambda: drained(et_v.at[pl.ds(0, 4)], el_send.at[zc]))
        pl.when(own_y)(lambda: drained(et_v.at[pl.ds(0, 6)], el_send.at[zc]))
        other = jnp.logical_not(own_x | own_y)
        pl.when(other)(lambda: drained(et_v.at[pl.ds(0, 8)], el_send.at[zc]))
    for n in range(2):
        along_z(n, lambda copy: copy.wait_send())
    for h in range(2):
        drained(kvr.at[h, most], kv_send.at[h])
        drained(gr.at[h, most], g_send.at[h])
        drained(gl.at[h, pl.ds(0, 7 * ROWS)], gl_send.at[h])
        drained(ps.at[h, pl.ds(0, 7)], c_send.at[h])
    att_out.wait()
    qg_out.wait()
    kwg_out.wait()
    vwg_out.wait()
    eg_out.wait()


def hand_over(*refs):
    given, results, held, sems = refs[:5], refs[5:10], refs[10:15], refs[15]
    inward = [pltpu.make_async_copy(given[i], held[i], sems.at[0, i]) for i in range(5)]
    outward = [pltpu.make_async_copy(held[i], results[i], sems.at[1, i]) for i in range(5)]
    for copy in inward:
        copy.start()
    for i in range(5):
        inward[i].wait()
        outward[i].start()
    for copy in outward:
        copy.wait()


def body(queries, enc_rows, key_weight, value_weight, enc_len, dec_len, route, out_grad):
    any_spec = pl.BlockSpec(memory_space=pl.ANY)
    dma = pltpu.SemaphoreType.DMA
    results = (
        jax.ShapeDtypeStruct((DEC, W2), BF),
        jax.ShapeDtypeStruct((DEC, W2), BF),
        jax.ShapeDtypeStruct((ROWS, W2), BF),
        jax.ShapeDtypeStruct((ROWS, W2), F32),
        jax.ShapeDtypeStruct((ROWS, W2), F32),
    )
    made = pl.pallas_call(
        kernel,
        out_shape=results,
        in_specs=[any_spec] * 8,
        out_specs=[any_spec] * 5,
        scratch_shapes=[
            pltpu.VMEM((32, 128, 128), BF),
            pltpu.VMEM((32, 128, 128), BF),
            pltpu.VMEM((NZ, W2, W2), BF),
            pltpu.VMEM((NZ, W2, W2), BF),
            pltpu.VMEM((DEC, W2), BF),
            pltpu.VMEM((DEC, W2), BF),
            pltpu.VMEM((ROWS, 2 * W2), F32),
            pltpu.VMEM((NDP * SLOT, ROWS), BF),
            pltpu.VMEM((ROWS, NDP * SLOT), BF),
            pltpu.VMEM((2, NDP * SLOT, W2), BF),
            pltpu.VMEM((2, NDP * SLOT, W2), BF),
            pltpu.VMEM((2, NDP * SLOT, W2), BF),
            pltpu.VMEM((2, NDP * SLOT, W2), BF),
            pltpu.VMEM((2, 2, ROWS, HD), BF),
            pltpu.VMEM((2, 8 * ROWS, HD), BF),
            pltpu.VMEM((8, 8, 128, 128), BF),
            pltpu.VMEM((2, 8, 128, HD), BF),
            pltpu.VMEM((2, 2, 4, 128, HD), BF),
            pltpu.VMEM((NZ, ROWS, W2), F32),
            pltpu.VMEM((2, 4, 4, ROWS, 128), BF),
            pltpu.VMEM((2, 4, 4, ROWS, 128), BF),
            pltpu.VMEM((DEC, W2), BF),
            pltpu.VMEM((DEC, W2), BF),
            pltpu.VMEM((ROWS, W2), BF),
            pltpu.VMEM((2, ROWS, W2), F32),
            pltpu.VMEM((1, NDP), jnp.int32),
            pltpu.VMEM((1, NDP), jnp.int32),
            pltpu.VMEM((1, NDP), jnp.int32),
            dma(()),
            dma((NZ, 2)),
            dma((2,)),
            dma((2, 4, 4)),
            dma((2, 4, 4)),
            dma((NZ,)),
            dma((NZ,)),
            dma((2,)),
            dma((2,)),
            dma((2,)),
            dma((2,)),
            dma((2,)),
            dma((2,)),
            dma((2,)),
            dma((2,)),
            dma((2,)),
            dma((2, 4, 4)),
            dma((2, 4, 4)),
            dma((5,)),
            dma((3,)),
        ],
        compiler_params=pltpu.CompilerParams(
            collective_id=0, has_side_effects=True, vmem_limit_bytes=60 * 1024 * 1024
        ),
    )(queries, enc_rows, key_weight, value_weight, enc_len, dec_len, route, out_grad)
    return pl.pallas_call(
        hand_over,
        out_shape=results,
        in_specs=[any_spec] * 5,
        out_specs=[any_spec] * 5,
        scratch_shapes=[pltpu.VMEM(r.shape, r.dtype) for r in results] + [dma((2, 5))],
        compiler_params=pltpu.CompilerParams(vmem_limit_bytes=60 * 1024 * 1024),
    )(*made)


def solution(mesh):
    in_specs = (
        P("dp", "mp"),
        P("dp", "mp"),
        P(None, "mp"),
        P(None, "mp"),
        P("dp", None),
        P("dp", None),
        P("dp", None),
        P("dp", "mp"),
    )
    out_specs = (P("dp", "mp"), P("dp", "mp"), P("dp", "mp"), P("dp", "mp"), P("dp", "mp"))
    return jax.shard_map(body, mesh=mesh, in_specs=in_specs, out_specs=out_specs, check_vma=False)
```

```python
import jax
import jax.numpy as jnp
from jax import lax
from jax.experimental import pallas as pl
from jax.experimental.pallas import tpu as pltpu
from jax.sharding import PartitionSpec as P

HD = 256
ROWS = 128
DEC = 256
SLOT = 16
NDP = 32
NZ = 8
W2 = 512
FAR = 3
DEAD = 65536.0
FARTHEST_FIRST = (10, 6, 9, 14, 11, 5, 8, 15, 2, 7, 13, 4, 1, 12, 3)
MESH = pl.DeviceIdType.MESH
BF = jnp.bfloat16
F32 = jnp.float32


def mm(a, b):
    return lax.dot_general(a, b, (((1,), (0,)), ((), ())), preferred_element_type=F32)


def mm_nt(a, b):
    return lax.dot_general(a, b, (((1,), (1,)), ((), ())), preferred_element_type=F32)


def mm_tn(a, b):
    return lax.dot_general(a, b, (((0,), (0,)), ((), ())), preferred_element_type=F32)


def iota(shape, dim):
    return lax.broadcasted_iota(jnp.int32, shape, dim)


def column_of(row, n):
    here = iota((n, n), 1)
    there = iota((n, n), 0)
    wide = jnp.broadcast_to(row, (n, n))
    col = jnp.sum(jnp.where(here == there, wide, 0.0), axis=1, keepdims=True)
    before = jnp.sum(jnp.where(here < there, wide, 0.0), axis=1, keepdims=True)
    return col, before


def kernel(
    q_hbm, enc_hbm, kw_hbm, vw_hbm, enc_len_hbm, dec_len_hbm, route_hbm, og_hbm,
    att_hbm, qg_hbm, eg_hbm, kwg_hbm, vwg_hbm,
    e_v, et_v, kw_v, vw_v, q_v, og_v, acc, oh_v, oht_v,
    slots, kvr, gs, gr, gsend, gl, el, ps, cr, dx, rs_s, rs_r,
    att_v, qg_v, eg_v, wg_v, enc_len, dec_len, route,
    enc_sem, w_sem, q_sem, z_send, z_recv, el_send, el_recv, elz_send,
    kv_send, kv_recv, g_send, g_recv, gl_send, gl_recv, c_send, c_recv,
    rs_send, rs_recv, out_sem, int_sem,
):
    d = lax.axis_index("dp")
    z = lax.axis_index("mp")
    x = d // 8
    y = (d // 2) % 4
    c = d % 2
    right = (d, (z + 1) % NZ)
    left = (d, (z + NZ - 1) % NZ)
    ring = (right, left)

    def chunk_at(n):
        off = jnp.where(n % 2 == 1, NZ - (n + 1) // 2, n // 2)
        return (z + off) % NZ

    def drained(buf, sem):
        pltpu.make_async_copy(buf, buf, sem).wait()

    for b in range(4):
        pltpu.make_async_copy(
            enc_hbm.at[:, pl.ds(b * 128, 128)], e_v.at[z * 4 + b], enc_sem
        ).start()

    barrier = pltpu.get_barrier_semaphore()
    for peer in (*ring, (d, (z + 2) % NZ), (d, (z + NZ - 2) % NZ)):
        pl.semaphore_signal(barrier, inc=1, device_id=peer, device_id_type=MESH)

    def greet(i, carry):
        pl.semaphore_signal(barrier, inc=1, device_id=((d + i) % NDP, z), device_id_type=MESH)
        return carry

    lax.fori_loop(1, NDP, greet, 0)

    def w_copy(zc, kv):
        src, dst = ((kw_hbm, kw_v), (vw_hbm, vw_v))[kv]
        return pltpu.make_async_copy(
            src.at[pl.ds(pl.multiple_of(zc * W2, W2), W2), :], dst.at[zc], w_sem.at[zc, kv]
        )

    def load_w(n, carry):
        zc = chunk_at(n)
        w_copy(zc, 0).start()
        w_copy(zc, 1).start()
        return carry

    int_copies = [
        pltpu.make_async_copy(src, dst, int_sem.at[i])
        for i, (src, dst) in enumerate(
            ((enc_len_hbm, enc_len), (route_hbm, route), (dec_len_hbm, dec_len))
        )
    ]
    for copy in int_copies:
        copy.start()

    pl.semaphore_wait(barrier, NDP + 3)
    pltpu.make_async_copy(e_v.at[pl.ds(0, 4)], e_v.at[pl.ds(z * 4, 4)], enc_sem).wait()

    def z_copy(direction, step, part):
        back = step - 1
        zc = (z + NZ - back) % NZ if direction == 0 else (z + back) % NZ
        at = zc * 4 + part
        return pltpu.make_async_remote_copy(
            src_ref=e_v.at[at],
            dst_ref=e_v.at[at],
            send_sem=z_send.at[direction, step - 1, part],
            recv_sem=z_recv.at[direction, step - 1, part],
            device_id=ring[direction],
            device_id_type=MESH,
        )

    def near(direction, part):
        return (part < 2) == (direction == 0)

    travel = ((0, 0), (1, 3), (0, 1), (1, 2), (0, 2), (1, 1), (0, 3), (1, 0))
    for direction, part in travel:
        z_copy(direction, 1, part).start()
    lax.fori_loop(0, NZ, load_w, 0)
    q_copy = pltpu.make_async_copy(q_hbm, q_v, q_sem.at[0])
    og_copy = pltpu.make_async_copy(og_hbm, og_v, q_sem.at[1])
    q_copy.start()
    og_copy.start()

    def to_line(zc, src, dst, device, here):
        @pl.when(here)
        def _():
            pltpu.make_async_copy(src, dst, el_recv.at[zc]).start()

        @pl.when(jnp.logical_not(here))
        def _():
            pltpu.make_async_remote_copy(
                src_ref=src, dst_ref=dst, send_sem=el_send.at[zc], recv_sem=el_recv.at[zc],
                device_id=device, device_id_type=MESH,
            ).start()

    int_copies[0].wait()
    int_copies[1].wait()
    lens_col, starts_col = column_of(enc_len[...].astype(F32), NDP)
    route_col, _ = column_of(route[...].astype(F32), NDP)
    pos = iota((NDP, ROWS), 1).astype(F32)
    inside = (pos >= starts_col) & (pos < starts_col + lens_col)
    dest = jnp.sum(
        jnp.where(inside, route_col * SLOT + pos - starts_col, 0.0), axis=0, keepdims=True
    )
    hot = iota((NDP * SLOT, ROWS), 0).astype(F32) == dest
    hot_f = jnp.where(hot, 1.0, 0.0)
    oh_v[...] = hot_f.astype(BF)

    acc[...] = jnp.zeros_like(acc)

    def process(zc):
        blocks = [e_v[zc * 4 + b] for b in range(4)]
        rows = jnp.concatenate(blocks, axis=1)
        w_copy(zc, 0).wait()
        w_copy(zc, 1).wait()
        acc[:, :W2] += mm(rows, kw_v[zc])
        acc[:, W2:] += mm(rows, vw_v[zc])
        for b in range(4):
            et_v[zc * 4 + b] = blocks[b].T

    def distribute(zc):
        xc = zc // 2
        half = zc % 2
        to_line(
            zc, et_v.at[pl.ds(zc * 4, 4)], el.at[c * 4 + x, pl.ds(half * 4, 4)],
            (xc * 8 + y * 2, z), (xc == x) & (c == 0),
        )
        for j in range(2):
            yc = half * 2 + j
            to_line(
                zc, et_v.at[pl.ds(zc * 4 + 2 * j, 2)], el.at[c * 4 + y, pl.ds(xc * 2, 2)],
                (x * 8 + yc * 2 + 1, z), (yc == y) & (c == 1),
            )

    process(z)
    distribute(z)

    def gather_step(k, carry):
        for direction, part in travel:
            z_copy(direction, k, part).wait_recv()
            if near(direction, part):
                z_copy(direction, k + 1, part).start()
            else:
                pl.when(k < 3)(z_copy(direction, k + 1, part).start)
        for zc in ((z + NZ - k) % NZ, (z + k) % NZ):
            process(zc)
            pl.when(k < FAR)(lambda: distribute(zc))
        return carry

    lax.fori_loop(1, 4, gather_step, 0)
    for direction, part in travel[:4]:
        z_copy(direction, 4, part).wait_recv()
    process((z + 4) % NZ)

    def line_blocks(zc, core):
        return pl.ds((zc % 2) * 4, 4) if core == 0 else pl.ds((zc // 2) * 2, 2)

    def on_holder(zc, fn):
        pl.when((c == 0) & (zc // 2 == x))(lambda: fn(0))
        pl.when((c == 1) & (zc % 2 == y // 2))(lambda: fn(1))

    def wait_line(zc):
        def one(core):
            drained(el.at[:, line_blocks(zc, core)], el_recv.at[zc])

        on_holder(zc, one)

    def along_z(n, act):
        zc, step, first, count = (
            (z + 2, 7, 0, 8), (z + 6, 1, 0, 8), (z + 2, 6, 4, 2), (z + 6, 2, 6, 2),
        )[n]
        zc = zc % NZ

        def one(core):
            at = el.at[pl.ds(first, count), line_blocks(zc, core)]
            act(pltpu.make_async_remote_copy(
                src_ref=at, dst_ref=at, send_sem=elz_send.at[n], recv_sem=el_recv.at[zc],
                device_id=(d, (z + step) % NZ), device_id_type=MESH,
            ))

        on_holder(zc, one)

    def exchange(src, dst, send_sem, recv_sem, h):
        mine = pl.ds(pl.multiple_of(d * SLOT, SLOT), SLOT)
        pltpu.make_async_copy(src.at[h, mine], dst.at[h, mine], recv_sem.at[h]).start()

        def send(i, carry):
            o = jnp.int32(0)
            for n in range(15):
                o = jnp.where(i // 2 == n, FARTHEST_FIRST[n], o)
            t = ((x + o // 4) % 4) * 8 + ((y + o % 4) % 4) * 2 + (c + i + 1) % 2
            pltpu.make_async_remote_copy(
                src_ref=src.at[h, pl.ds(pl.multiple_of(t * SLOT, SLOT), SLOT)],
                dst_ref=dst.at[h, mine],
                send_sem=send_sem.at[h],
                recv_sem=recv_sem.at[h],
                device_id=(t, z),
                device_id_type=MESH,
            ).start()
            return carry

        lax.fori_loop(0, NDP - 1, send, 0)

    most = pl.ds(0, (NDP - 1) * SLOT)
    hot_b = oh_v[...]
    dead = jnp.sum(hot_b.astype(F32), axis=1, keepdims=True) < 0.5
    for h in range(2):
        cols = pl.ds(h * HD, HD)
        keys = mm(hot_b, acc[:, cols].astype(BF))
        slots[h, :, :HD] = jnp.where(dead, DEAD, keys).astype(BF)
        slots[h, :, HD:] = mm(hot_b, acc[:, pl.ds(W2 + h * HD, HD)].astype(BF)).astype(BF)
        exchange(slots, kvr, kv_send, kv_recv, h)
    pl.when(c == 0)(lambda: distribute((z + 4) % NZ))

    def relay():
        for k in (2, 6):
            wait_line((z + k) % NZ)
        for n in range(4):
            along_z(n, lambda copy: copy.start())


    relay()
    oht_v[...] = hot_b.T

    n_keys = NDP * SLOT
    int_copies[2].wait()
    dec_col, dec_before = column_of(dec_len[...].astype(F32), NDP)
    same = iota((NDP, n_keys), 1) // SLOT == iota((NDP, n_keys), 0)
    first = jnp.sum(jnp.where(same, dec_before, 0.0), axis=0, keepdims=True)
    last = jnp.sum(jnp.where(same, dec_before + dec_col, 0.0), axis=0, keepdims=True)
    row = iota((DEC, n_keys), 0).astype(F32)
    own = (row >= first) & (row < last)
    q_copy.wait()
    og_copy.wait()
    for h in range(2):
        cols = pl.ds(h * HD, HD)
        drained(kvr.at[h], kv_recv.at[h])
        q = q_v[:, cols]
        g = og_v[:, cols]
        k = kvr[h, :, :HD]
        v = kvr[h, :, HD:]
        total = mm_nt(jnp.ones((16, HD), BF), k)[:1]
        allowed = own & (total < 4.0e6)
        s = jnp.where(allowed, mm_nt(q, k) * (HD ** -0.5), -1e30)
        top = jnp.max(s, axis=1, keepdims=True)
        expo = jnp.exp(s - top)
        probs = expo * (1.0 / jnp.sum(expo, axis=1, keepdims=True))
        weights = probs.astype(BF)
        dw = mm_nt(g, v)
        delta = jnp.sum(probs * dw, axis=1, keepdims=True)
        ds = (probs * (dw - delta) * (HD ** -0.5)).astype(BF)
        gs[h, :, :HD] = mm_tn(ds, q).astype(BF)
        gs[h, :, HD:] = mm_tn(weights, g).astype(BF)
        exchange(gs, gr, g_send, g_recv, h)
        att_v[:, cols] = mm(weights, v).astype(BF)
        qg_v[:, cols] = mm(ds, k).astype(BF)
    att_out = pltpu.make_async_copy(att_v, att_hbm, out_sem.at[0])
    qg_out = pltpu.make_async_copy(qg_v, qg_hbm, out_sem.at[1])
    att_out.start()
    qg_out.start()

    def spread(h):
        def one(kv, i):
            if kv == 0:
                t = ((x + i) % 4) * 8 + y * 2
                at = c * 4 + x
            else:
                t = x * 8 + ((y + i) % 4) * 2 + 1
                at = c * 4 + y
            src = gsend.at[h, kv]
            dst = gl.at[h, pl.ds(pl.multiple_of(at * ROWS, ROWS), ROWS)]

            def far():
                pltpu.make_async_remote_copy(
                    src_ref=src, dst_ref=dst, send_sem=gl_send.at[h], recv_sem=gl_recv.at[h],
                    device_id=(t, z), device_id_type=MESH,
                ).start()

            if i > 0:
                far()
            else:
                pl.when(c != kv)(far)

                @pl.when(c == kv)
                def _():
                    pltpu.make_async_copy(src, dst, gl_recv.at[h]).start()

        for i in (2, 1, 3, 0):
            one(0, i)
            one(1, i)

    def unpack(h):
        drained(gr.at[h], g_recv.at[h])
        rows = mm(oht_v[...], gr[h]).astype(BF)
        gsend[h, 0] = rows[:, :HD]
        gsend[h, 1] = rows[:, HD:]
        spread(h)

    def back(h, zc):
        cols = pl.ds(h * HD, HD)
        return mm_nt(gsend[h, 0], kw_v[zc, :, cols]) + mm_nt(gsend[h, 1], vw_v[zc, :, cols])

    def send_block(h, b):
        t = jnp.where(c == 0, x * 8 + b, (b // 2) * 8 + y * 2 + b % 2)
        dst = cr.at[h, c, jnp.where(c == 0, y, x)]

        @pl.when(t == d)
        def _():
            pltpu.make_async_copy(ps.at[h, b], dst, c_recv.at[h]).start()

        @pl.when(t != d)
        def _():
            pltpu.make_async_remote_copy(
                src_ref=ps.at[h, b], dst_ref=dst, send_sem=c_send.at[h], recv_sem=c_recv.at[h],
                device_id=(t, z), device_id_type=MESH,
            ).start()

    def partial_blocks(h):
        drained(gl.at[h], gl_recv.at[h])

        def blocks(n, carry):
            lhs = jnp.concatenate(
                [
                    jnp.concatenate([el[j, n * 4 + i] for j in range(8)], axis=1)
                    for i in range(4)
                ],
                axis=0,
            )
            out = mm(lhs, gl[h]).astype(BF)
            for i in range(4):
                ps[h, n * 4 + i] = out[i * 128:(i + 1) * 128]
                send_block(h, n * 4 + i)
            return carry

        lax.fori_loop(0, 2, blocks, 0)

    unpack(0)

    def back_first(zc, carry):
        dx[zc] = back(0, zc)
        return carry

    lax.fori_loop(0, NZ, back_first, 0)
    unpack(1)

    def rs_copy(direction, step, part):
        return pltpu.make_async_remote_copy(
            src_ref=rs_s.at[direction, step - 1, part],
            dst_ref=rs_r.at[direction, step - 1, part],
            send_sem=rs_send.at[direction, step - 1, part],
            recv_sem=rs_recv.at[direction, step - 1, part],
            device_id=ring[direction],
            device_id_type=MESH,
        )

    def rs_part(step, direction, part):
        far = 5 - step
        zc = (z + far) % NZ if direction == 0 else (z + NZ - far) % NZ
        term = dx[zc, :, pl.ds(part * 128, 128)]
        if step >= 3 or (step == 2 and near(direction, part)):
            rs_copy(direction, step - 1, part).wait_recv()
            term = term + rs_r[direction, step - 2, part].astype(F32)
        rs_s[direction, step - 1, part] = term.astype(BF)
        rs_copy(direction, step, part).start()

    def back_second(n, carry):
        zc = chunk_at(7 - n)
        dx[zc] += back(1, zc)
        return carry

    first_parts, last_parts = travel[:4], travel[4:]
    lax.fori_loop(0, 1, back_second, 0)
    for direction, part in first_parts:
        rs_part(1, direction, part)
    lax.fori_loop(1, 3, back_second, 0)
    for direction, part in last_parts:
        rs_part(2, direction, part)
    lax.fori_loop(3, NZ, back_second, 0)
    for k in (0, 1, 7, 3, 5, 4):
        wait_line((z + k) % NZ)
    partial_blocks(0)
    for direction, part in first_parts:
        rs_part(2, direction, part)
    partial_blocks(1)
    for step in (3, 4):
        for direction, part in last_parts + first_parts:
            rs_part(step, direction, part)

    for h in range(2):
        drained(cr.at[h], c_recv.at[h])
        cols = pl.ds(h * HD, HD)
        for kv in range(2):
            total = cr[h, kv, 0].astype(F32)
            for j in range(1, 4):
                total = total + cr[h, kv, j].astype(F32)
            wg_v[kv, :, cols] = total
    kwg_out = pltpu.make_async_copy(wg_v.at[0], kwg_hbm, out_sem.at[2])
    vwg_out = pltpu.make_async_copy(wg_v.at[1], vwg_hbm, out_sem.at[3])
    kwg_out.start()
    vwg_out.start()
    for part in (2, 1, 3, 0):
        cols = pl.ds(part * 128, 128)
        total = dx[z, :, cols]
        for direction in range(2):
            rs_copy(direction, 4, part).wait_recv()
            total = total + rs_r[direction, 3, part].astype(F32)
        eg_v[:, cols] = total.astype(BF)
    eg_out = pltpu.make_async_copy(eg_v, eg_hbm, out_sem.at[4])
    eg_out.start()

    for direction in range(2):
        for step in range(1, 5):
            for part in range(4):
                if step < 4 or near(direction, part):
                    z_copy(direction, step, part).wait_send()
                if step > 1 or near(direction, part):
                    rs_copy(direction, step, part).wait_send()
    for k in (0, 1, 7, 2, 6, 4):
        zc = (z + k) % NZ
        own_x = (c == 0) & (zc // 2 == x)
        own_y = (c == 1) & (zc % 2 == y // 2)
        sent = (c == 0) | (k != 4)
        other = jnp.logical_not(own_x | own_y)
        pl.when(sent & own_x)(lambda: drained(et_v.at[pl.ds(0, 4)], el_send.at[zc]))
        pl.when(sent & own_y)(lambda: drained(et_v.at[pl.ds(0, 6)], el_send.at[zc]))
        pl.when(sent & other)(lambda: drained(et_v.at[pl.ds(0, 8)], el_send.at[zc]))
    for n in range(4):
        along_z(n, lambda copy: copy.wait_send())
    for h in range(2):
        drained(kvr.at[h, most], kv_send.at[h])
        drained(gr.at[h, most], g_send.at[h])
        drained(gl.at[h, pl.ds(0, 7 * ROWS)], gl_send.at[h])
        drained(ps.at[h, pl.ds(0, 7)], c_send.at[h])
    att_out.wait()
    qg_out.wait()
    kwg_out.wait()
    vwg_out.wait()
    eg_out.wait()


def hand_over(*refs):
    given, results, held, sems = refs[:5], refs[5:10], refs[10:15], refs[15]
    inward = [pltpu.make_async_copy(given[i], held[i], sems.at[0, i]) for i in range(5)]
    outward = [pltpu.make_async_copy(held[i], results[i], sems.at[1, i]) for i in range(5)]
    for copy in inward:
        copy.start()
    for i in range(5):
        inward[i].wait()
        outward[i].start()
    for copy in outward:
        copy.wait()


def body(queries, enc_rows, key_weight, value_weight, enc_len, dec_len, route, out_grad):
    any_spec = pl.BlockSpec(memory_space=pl.ANY)
    dma = pltpu.SemaphoreType.DMA
    results = (
        jax.ShapeDtypeStruct((DEC, W2), BF),
        jax.ShapeDtypeStruct((DEC, W2), BF),
        jax.ShapeDtypeStruct((ROWS, W2), BF),
        jax.ShapeDtypeStruct((ROWS, W2), F32),
        jax.ShapeDtypeStruct((ROWS, W2), F32),
    )
    made = pl.pallas_call(
        kernel,
        out_shape=results,
        in_specs=[any_spec] * 8,
        out_specs=[any_spec] * 5,
        scratch_shapes=[
            pltpu.VMEM((32, 128, 128), BF),
            pltpu.VMEM((32, 128, 128), BF),
            pltpu.VMEM((NZ, W2, W2), BF),
            pltpu.VMEM((NZ, W2, W2), BF),
            pltpu.VMEM((DEC, W2), BF),
            pltpu.VMEM((DEC, W2), BF),
            pltpu.VMEM((ROWS, 2 * W2), F32),
            pltpu.VMEM((NDP * SLOT, ROWS), BF),
            pltpu.VMEM((ROWS, NDP * SLOT), BF),
            pltpu.VMEM((2, NDP * SLOT, W2), BF),
            pltpu.VMEM((2, NDP * SLOT, W2), BF),
            pltpu.VMEM((2, NDP * SLOT, W2), BF),
            pltpu.VMEM((2, NDP * SLOT, W2), BF),
            pltpu.VMEM((2, 2, ROWS, HD), BF),
            pltpu.VMEM((2, 8 * ROWS, HD), BF),
            pltpu.VMEM((8, 8, 128, 128), BF),
            pltpu.VMEM((2, 8, 128, HD), BF),
            pltpu.VMEM((2, 2, 4, 128, HD), BF),
            pltpu.VMEM((NZ, ROWS, W2), F32),
            pltpu.VMEM((2, 4, 4, ROWS, 128), BF),
            pltpu.VMEM((2, 4, 4, ROWS, 128), BF),
            pltpu.VMEM((DEC, W2), BF),
            pltpu.VMEM((DEC, W2), BF),
            pltpu.VMEM((ROWS, W2), BF),
            pltpu.VMEM((2, ROWS, W2), F32),
            pltpu.VMEM((1, NDP), jnp.int32),
            pltpu.VMEM((1, NDP), jnp.int32),
            pltpu.VMEM((1, NDP), jnp.int32),
            dma(()),
            dma((NZ, 2)),
            dma((2,)),
            dma((2, 4, 4)),
            dma((2, 4, 4)),
            dma((NZ,)),
            dma((NZ,)),
            dma((4,)),
            dma((2,)),
            dma((2,)),
            dma((2,)),
            dma((2,)),
            dma((2,)),
            dma((2,)),
            dma((2,)),
            dma((2,)),
            dma((2, 4, 4)),
            dma((2, 4, 4)),
            dma((5,)),
            dma((3,)),
        ],
        compiler_params=pltpu.CompilerParams(
            collective_id=0, has_side_effects=True, vmem_limit_bytes=60 * 1024 * 1024
        ),
    )(queries, enc_rows, key_weight, value_weight, enc_len, dec_len, route, out_grad)
    return pl.pallas_call(
        hand_over,
        out_shape=results,
        in_specs=[any_spec] * 5,
        out_specs=[any_spec] * 5,
        scratch_shapes=[pltpu.VMEM(r.shape, r.dtype) for r in results] + [dma((2, 5))],
        compiler_params=pltpu.CompilerParams(vmem_limit_bytes=60 * 1024 * 1024),
    )(*made)


def solution(mesh):
    in_specs = (
        P("dp", "mp"),
        P("dp", "mp"),
        P(None, "mp"),
        P(None, "mp"),
        P("dp", None),
        P("dp", None),
        P("dp", None),
        P("dp", "mp"),
    )
    out_specs = (P("dp", "mp"), P("dp", "mp"), P("dp", "mp"), P("dp", "mp"), P("dp", "mp"))
    return jax.shard_map(body, mesh=mesh, in_specs=in_specs, out_specs=out_specs, check_vma=False)
```

```python
import jax
import jax.numpy as jnp
from jax import lax
from jax.experimental import pallas as pl
from jax.experimental.pallas import tpu as pltpu
from jax.sharding import PartitionSpec as P

HD = 256
ROWS = 128
DEC = 256
SLOT = 16
NDP = 32
NZ = 8
W2 = 512
FAR = 3
DEAD = 65536.0
FARTHEST_FIRST = (10, 6, 9, 14, 11, 5, 8, 15, 2, 7, 13, 4, 1, 12, 3)
MESH = pl.DeviceIdType.MESH
BF = jnp.bfloat16
F32 = jnp.float32


def mm(a, b):
    return lax.dot_general(a, b, (((1,), (0,)), ((), ())), preferred_element_type=F32)


def mm_nt(a, b):
    return lax.dot_general(a, b, (((1,), (1,)), ((), ())), preferred_element_type=F32)


def mm_tn(a, b):
    return lax.dot_general(a, b, (((0,), (0,)), ((), ())), preferred_element_type=F32)


def iota(shape, dim):
    return lax.broadcasted_iota(jnp.int32, shape, dim)


def column_of(row, n):
    here = iota((n, n), 1)
    there = iota((n, n), 0)
    wide = jnp.broadcast_to(row, (n, n))
    col = jnp.sum(jnp.where(here == there, wide, 0.0), axis=1, keepdims=True)
    before = jnp.sum(jnp.where(here < there, wide, 0.0), axis=1, keepdims=True)
    return col, before


def kernel(
    q_hbm, enc_hbm, kw_hbm, vw_hbm, enc_len_hbm, dec_len_hbm, route_hbm, og_hbm,
    att_hbm, qg_hbm, eg_hbm, kwg_hbm, vwg_hbm,
    e_v, et_v, kw_v, vw_v, q_v, og_v, acc, oh_v, oht_v,
    slots, kvr, gs, gr, gsend, gl, el, ps, cr, dx, rs_s, rs_r,
    att_v, qg_v, eg_v, wg_v, enc_len, dec_len, route,
    enc_sem, w_sem, q_sem, z_send, z_recv, el_send, el_recv, elz_send,
    kv_send, kv_recv, g_send, g_recv, gl_send, gl_recv, c_send, c_recv,
    rs_send, rs_recv, out_sem, int_sem,
):
    d = lax.axis_index("dp")
    z = lax.axis_index("mp")
    x = d // 8
    y = (d // 2) % 4
    c = d % 2
    right = (d, (z + 1) % NZ)
    left = (d, (z + NZ - 1) % NZ)
    ring = (right, left)

    def chunk_at(n):
        off = jnp.where(n % 2 == 1, NZ - (n + 1) // 2, n // 2)
        return (z + off) % NZ

    def drained(buf, sem):
        pltpu.make_async_copy(buf, buf, sem).wait()

    for b in range(4):
        pltpu.make_async_copy(
            enc_hbm.at[:, pl.ds(b * 128, 128)], e_v.at[z * 4 + b], enc_sem
        ).start()

    barrier = pltpu.get_barrier_semaphore()
    for peer in (*ring, (d, (z + 2) % NZ), (d, (z + NZ - 2) % NZ)):
        pl.semaphore_signal(barrier, inc=1, device_id=peer, device_id_type=MESH)

    def greet(i, carry):
        pl.semaphore_signal(barrier, inc=1, device_id=((d + i) % NDP, z), device_id_type=MESH)
        return carry

    lax.fori_loop(1, NDP, greet, 0)

    def w_copy(zc, kv):
        src, dst = ((kw_hbm, kw_v), (vw_hbm, vw_v))[kv]
        return pltpu.make_async_copy(
            src.at[pl.ds(pl.multiple_of(zc * W2, W2), W2), :], dst.at[zc], w_sem.at[zc, kv]
        )

    def load_w(n, carry):
        zc = chunk_at(n)
        w_copy(zc, 0).start()
        w_copy(zc, 1).start()
        return carry

    int_copies = [
        pltpu.make_async_copy(src, dst, int_sem.at[i])
        for i, (src, dst) in enumerate(
            ((enc_len_hbm, enc_len), (route_hbm, route), (dec_len_hbm, dec_len))
        )
    ]
    for copy in int_copies:
        copy.start()

    pl.semaphore_wait(barrier, NDP + 3)
    pltpu.make_async_copy(e_v.at[pl.ds(0, 4)], e_v.at[pl.ds(z * 4, 4)], enc_sem).wait()

    def z_copy(direction, step, part):
        back = step - 1
        zc = (z + NZ - back) % NZ if direction == 0 else (z + back) % NZ
        at = zc * 4 + part
        return pltpu.make_async_remote_copy(
            src_ref=e_v.at[at],
            dst_ref=e_v.at[at],
            send_sem=z_send.at[direction, step - 1, part],
            recv_sem=z_recv.at[direction, step - 1, part],
            device_id=ring[direction],
            device_id_type=MESH,
        )

    def near(direction, part):
        return (part < 2) == (direction == 0)

    travel = ((0, 0), (1, 3), (0, 1), (1, 2), (0, 2), (1, 1), (0, 3), (1, 0))
    for direction, part in travel:
        z_copy(direction, 1, part).start()
    lax.fori_loop(0, NZ, load_w, 0)
    q_copy = pltpu.make_async_copy(q_hbm, q_v, q_sem.at[0])
    og_copy = pltpu.make_async_copy(og_hbm, og_v, q_sem.at[1])
    q_copy.start()
    og_copy.start()

    def to_line(zc, src, dst, device, here):
        @pl.when(here)
        def _():
            pltpu.make_async_copy(src, dst, el_recv.at[zc]).start()

        @pl.when(jnp.logical_not(here))
        def _():
            pltpu.make_async_remote_copy(
                src_ref=src, dst_ref=dst, send_sem=el_send.at[zc], recv_sem=el_recv.at[zc],
                device_id=device, device_id_type=MESH,
            ).start()

    int_copies[0].wait()
    int_copies[1].wait()
    lens_col, starts_col = column_of(enc_len[...].astype(F32), NDP)
    route_col, _ = column_of(route[...].astype(F32), NDP)
    pos = iota((NDP, ROWS), 1).astype(F32)
    inside = (pos >= starts_col) & (pos < starts_col + lens_col)
    dest = jnp.sum(
        jnp.where(inside, route_col * SLOT + pos - starts_col, 0.0), axis=0, keepdims=True
    )
    hot = iota((NDP * SLOT, ROWS), 0).astype(F32) == dest
    hot_f = jnp.where(hot, 1.0, 0.0)
    oh_v[...] = hot_f.astype(BF)

    acc[...] = jnp.zeros_like(acc)

    def process(zc):
        blocks = [e_v[zc * 4 + b] for b in range(4)]
        rows = jnp.concatenate(blocks, axis=1)
        w_copy(zc, 0).wait()
        w_copy(zc, 1).wait()
        acc[:, :W2] += mm(rows, kw_v[zc])
        acc[:, W2:] += mm(rows, vw_v[zc])

    def turn(zc):
        for b in range(4):
            et_v[zc * 4 + b] = e_v[zc * 4 + b].T

    def distribute(zc):
        xc = zc // 2
        half = zc % 2
        to_line(
            zc, et_v.at[pl.ds(zc * 4, 4)], el.at[c * 4 + x, pl.ds(half * 4, 4)],
            (xc * 8 + y * 2, z), (xc == x) & (c == 0),
        )
        for j in range(2):
            yc = half * 2 + j
            to_line(
                zc, et_v.at[pl.ds(zc * 4 + 2 * j, 2)], el.at[c * 4 + y, pl.ds(xc * 2, 2)],
                (x * 8 + yc * 2 + 1, z), (yc == y) & (c == 1),
            )

    process(z)
    turn(z)
    distribute(z)

    def gather_step(k, carry):
        for direction, part in travel:
            z_copy(direction, k, part).wait_recv()
            if near(direction, part):
                z_copy(direction, k + 1, part).start()
            else:
                pl.when(k < 3)(z_copy(direction, k + 1, part).start)
        for zc in ((z + NZ - k) % NZ, (z + k) % NZ):
            process(zc)
            turn(zc)
            pl.when(k < FAR)(lambda: distribute(zc))
        return carry

    lax.fori_loop(1, 4, gather_step, 0)
    for direction, part in travel[:4]:
        z_copy(direction, 4, part).wait_recv()
    process((z + 4) % NZ)

    def line_blocks(zc, core):
        return pl.ds((zc % 2) * 4, 4) if core == 0 else pl.ds((zc // 2) * 2, 2)

    def on_holder(zc, fn):
        pl.when((c == 0) & (zc // 2 == x))(lambda: fn(0))
        pl.when((c == 1) & (zc % 2 == y // 2))(lambda: fn(1))

    def wait_line(zc):
        def one(core):
            drained(el.at[:, line_blocks(zc, core)], el_recv.at[zc])

        on_holder(zc, one)

    def along_z(n, act):
        zc, step, first, count = (
            (z + 2, 7, 0, 8), (z + 6, 1, 0, 8), (z + 2, 6, 4, 2), (z + 6, 2, 6, 2),
        )[n]
        zc = zc % NZ

        def one(core):
            at = el.at[pl.ds(first, count), line_blocks(zc, core)]
            act(pltpu.make_async_remote_copy(
                src_ref=at, dst_ref=at, send_sem=elz_send.at[n], recv_sem=el_recv.at[zc],
                device_id=(d, (z + step) % NZ), device_id_type=MESH,
            ))

        on_holder(zc, one)

    def exchange(src, dst, send_sem, recv_sem, h):
        mine = pl.ds(pl.multiple_of(d * SLOT, SLOT), SLOT)
        pltpu.make_async_copy(src.at[h, mine], dst.at[h, mine], recv_sem.at[h]).start()

        def send(i, carry):
            o = jnp.int32(0)
            for n in range(15):
                o = jnp.where(i // 2 == n, FARTHEST_FIRST[n], o)
            t = ((x + o // 4) % 4) * 8 + ((y + o % 4) % 4) * 2 + (c + i + 1) % 2
            pltpu.make_async_remote_copy(
                src_ref=src.at[h, pl.ds(pl.multiple_of(t * SLOT, SLOT), SLOT)],
                dst_ref=dst.at[h, mine],
                send_sem=send_sem.at[h],
                recv_sem=recv_sem.at[h],
                device_id=(t, z),
                device_id_type=MESH,
            ).start()
            return carry

        lax.fori_loop(0, NDP - 1, send, 0)

    most = pl.ds(0, (NDP - 1) * SLOT)
    hot_b = oh_v[...]
    dead = jnp.sum(hot_b.astype(F32), axis=1, keepdims=True) < 0.5
    for h in range(2):
        cols = pl.ds(h * HD, HD)
        keys = mm(hot_b, acc[:, cols].astype(BF))
        slots[h, :, :HD] = jnp.where(dead, DEAD, keys).astype(BF)
        slots[h, :, HD:] = mm(hot_b, acc[:, pl.ds(W2 + h * HD, HD)].astype(BF)).astype(BF)
        exchange(slots, kvr, kv_send, kv_recv, h)
    turn((z + 4) % NZ)
    pl.when(c == 0)(lambda: distribute((z + 4) % NZ))

    def relay():
        for k in (2, 6):
            wait_line((z + k) % NZ)
        for n in range(4):
            along_z(n, lambda copy: copy.start())


    relay()
    oht_v[...] = hot_b.T

    n_keys = NDP * SLOT
    int_copies[2].wait()
    dec_col, dec_before = column_of(dec_len[...].astype(F32), NDP)
    same = iota((NDP, n_keys), 1) // SLOT == iota((NDP, n_keys), 0)
    first = jnp.sum(jnp.where(same, dec_before, 0.0), axis=0, keepdims=True)
    last = jnp.sum(jnp.where(same, dec_before + dec_col, 0.0), axis=0, keepdims=True)
    row = iota((DEC, n_keys), 0).astype(F32)
    own = (row >= first) & (row < last)
    q_copy.wait()
    og_copy.wait()
    for h in range(2):
        cols = pl.ds(h * HD, HD)
        drained(kvr.at[h], kv_recv.at[h])
        q = q_v[:, cols]
        g = og_v[:, cols]
        k = kvr[h, :, :HD]
        v = kvr[h, :, HD:]
        total = mm_nt(jnp.ones((16, HD), BF), k)[:1]
        allowed = own & (total < 4.0e6)
        s = jnp.where(allowed, mm_nt(q, k) * (HD ** -0.5), -1e30)
        top = jnp.max(s, axis=1, keepdims=True)
        expo = jnp.exp(s - top)
        probs = expo * (1.0 / jnp.sum(expo, axis=1, keepdims=True))
        weights = probs.astype(BF)
        dw = mm_nt(g, v)
        delta = jnp.sum(probs * dw, axis=1, keepdims=True)
        ds = (probs * (dw - delta) * (HD ** -0.5)).astype(BF)
        gs[h, :, :HD] = mm_tn(ds, q).astype(BF)
        gs[h, :, HD:] = mm_tn(weights, g).astype(BF)
        exchange(gs, gr, g_send, g_recv, h)
        att_v[:, cols] = mm(weights, v).astype(BF)
        qg_v[:, cols] = mm(ds, k).astype(BF)
    att_out = pltpu.make_async_copy(att_v, att_hbm, out_sem.at[0])
    qg_out = pltpu.make_async_copy(qg_v, qg_hbm, out_sem.at[1])
    att_out.start()
    qg_out.start()

    def spread(h):
        def one(kv, i):
            if kv == 0:
                t = ((x + i) % 4) * 8 + y * 2
                at = c * 4 + x
            else:
                t = x * 8 + ((y + i) % 4) * 2 + 1
                at = c * 4 + y
            src = gsend.at[h, kv]
            dst = gl.at[h, pl.ds(pl.multiple_of(at * ROWS, ROWS), ROWS)]

            def far():
                pltpu.make_async_remote_copy(
                    src_ref=src, dst_ref=dst, send_sem=gl_send.at[h], recv_sem=gl_recv.at[h],
                    device_id=(t, z), device_id_type=MESH,
                ).start()

            if i > 0:
                far()
            else:
                pl.when(c != kv)(far)

                @pl.when(c == kv)
                def _():
                    pltpu.make_async_copy(src, dst, gl_recv.at[h]).start()

        for i in (2, 1, 3, 0):
            one(0, i)
            one(1, i)

    def unpack(h):
        drained(gr.at[h], g_recv.at[h])
        rows = mm(oht_v[...], gr[h]).astype(BF)
        gsend[h, 0] = rows[:, :HD]
        gsend[h, 1] = rows[:, HD:]
        spread(h)

    def back(h, zc):
        cols = pl.ds(h * HD, HD)
        grads = jnp.concatenate([gsend[h, 0], gsend[h, 1]], axis=1)
        weights = jnp.concatenate([kw_v[zc, :, cols], vw_v[zc, :, cols]], axis=1)
        return mm_nt(grads, weights)

    def send_block(h, b):
        t = jnp.where(c == 0, x * 8 + b, (b // 2) * 8 + y * 2 + b % 2)
        dst = cr.at[h, c, jnp.where(c == 0, y, x)]

        @pl.when(t == d)
        def _():
            pltpu.make_async_copy(ps.at[h, b], dst, c_recv.at[h]).start()

        @pl.when(t != d)
        def _():
            pltpu.make_async_remote_copy(
                src_ref=ps.at[h, b], dst_ref=dst, send_sem=c_send.at[h], recv_sem=c_recv.at[h],
                device_id=(t, z), device_id_type=MESH,
            ).start()

    def partial_blocks(h):
        drained(gl.at[h], gl_recv.at[h])

        def blocks(n, carry):
            lhs = jnp.concatenate(
                [
                    jnp.concatenate([el[j, n * 4 + i] for j in range(8)], axis=1)
                    for i in range(4)
                ],
                axis=0,
            )
            out = mm(lhs, gl[h]).astype(BF)
            for i in range(4):
                ps[h, n * 4 + i] = out[i * 128:(i + 1) * 128]
                send_block(h, n * 4 + i)
            return carry

        lax.fori_loop(0, 2, blocks, 0)

    unpack(0)

    def back_first(zc, carry):
        dx[zc] = back(0, zc)
        return carry

    lax.fori_loop(0, NZ, back_first, 0)
    unpack(1)

    def rs_copy(direction, step, part):
        return pltpu.make_async_remote_copy(
            src_ref=rs_s.at[direction, step - 1, part],
            dst_ref=rs_r.at[direction, step - 1, part],
            send_sem=rs_send.at[direction, step - 1, part],
            recv_sem=rs_recv.at[direction, step - 1, part],
            device_id=ring[direction],
            device_id_type=MESH,
        )

    def rs_part(step, direction, part):
        far = 5 - step
        zc = (z + far) % NZ if direction == 0 else (z + NZ - far) % NZ
        term = dx[zc, :, pl.ds(part * 128, 128)]
        if step >= 3 or (step == 2 and near(direction, part)):
            rs_copy(direction, step - 1, part).wait_recv()
            term = term + rs_r[direction, step - 2, part].astype(F32)
        rs_s[direction, step - 1, part] = term.astype(BF)
        rs_copy(direction, step, part).start()

    def back_second(n, carry):
        zc = chunk_at(7 - n)
        dx[zc] += back(1, zc)
        return carry

    first_parts, last_parts = travel[:4], travel[4:]
    lax.fori_loop(0, 1, back_second, 0)
    for direction, part in first_parts:
        rs_part(1, direction, part)
    lax.fori_loop(1, 3, back_second, 0)
    for direction, part in last_parts:
        rs_part(2, direction, part)
    lax.fori_loop(3, NZ, back_second, 0)
    for k in (0, 1, 7, 3, 5, 4):
        wait_line((z + k) % NZ)
    partial_blocks(0)
    for direction, part in first_parts:
        rs_part(2, direction, part)
    partial_blocks(1)
    for step in (3, 4):
        for direction, part in last_parts + first_parts:
            rs_part(step, direction, part)

    for h in range(2):
        drained(cr.at[h], c_recv.at[h])
        cols = pl.ds(h * HD, HD)
        for kv in range(2):
            total = cr[h, kv, 0].astype(F32)
            for j in range(1, 4):
                total = total + cr[h, kv, j].astype(F32)
            wg_v[kv, :, cols] = total
    kwg_out = pltpu.make_async_copy(wg_v.at[0], kwg_hbm, out_sem.at[2])
    vwg_out = pltpu.make_async_copy(wg_v.at[1], vwg_hbm, out_sem.at[3])
    kwg_out.start()
    vwg_out.start()
    for part in (2, 1, 3, 0):
        cols = pl.ds(part * 128, 128)
        total = dx[z, :, cols]
        for direction in range(2):
            rs_copy(direction, 4, part).wait_recv()
            total = total + rs_r[direction, 3, part].astype(F32)
        eg_v[:, cols] = total.astype(BF)
    eg_out = pltpu.make_async_copy(eg_v, eg_hbm, out_sem.at[4])
    eg_out.start()

    for direction in range(2):
        for step in range(1, 5):
            for part in range(4):
                if step < 4 or near(direction, part):
                    z_copy(direction, step, part).wait_send()
                if step > 1 or near(direction, part):
                    rs_copy(direction, step, part).wait_send()
    for k in (0, 1, 7, 2, 6, 4):
        zc = (z + k) % NZ
        own_x = (c == 0) & (zc // 2 == x)
        own_y = (c == 1) & (zc % 2 == y // 2)
        sent = (c == 0) | (k != 4)
        other = jnp.logical_not(own_x | own_y)
        pl.when(sent & own_x)(lambda: drained(et_v.at[pl.ds(0, 4)], el_send.at[zc]))
        pl.when(sent & own_y)(lambda: drained(et_v.at[pl.ds(0, 6)], el_send.at[zc]))
        pl.when(sent & other)(lambda: drained(et_v.at[pl.ds(0, 8)], el_send.at[zc]))
    for n in range(4):
        along_z(n, lambda copy: copy.wait_send())
    for h in range(2):
        drained(kvr.at[h, most], kv_send.at[h])
        drained(gr.at[h, most], g_send.at[h])
        drained(gl.at[h, pl.ds(0, 7 * ROWS)], gl_send.at[h])
        drained(ps.at[h, pl.ds(0, 7)], c_send.at[h])
    att_out.wait()
    qg_out.wait()
    kwg_out.wait()
    vwg_out.wait()
    eg_out.wait()


def hand_over(*refs):
    given, results, held, sems = refs[:5], refs[5:10], refs[10:15], refs[15]
    inward = [pltpu.make_async_copy(given[i], held[i], sems.at[0, i]) for i in range(5)]
    outward = [pltpu.make_async_copy(held[i], results[i], sems.at[1, i]) for i in range(5)]
    for copy in inward:
        copy.start()
    for i in range(5):
        inward[i].wait()
        outward[i].start()
    for copy in outward:
        copy.wait()


def body(queries, enc_rows, key_weight, value_weight, enc_len, dec_len, route, out_grad):
    any_spec = pl.BlockSpec(memory_space=pl.ANY)
    dma = pltpu.SemaphoreType.DMA
    results = (
        jax.ShapeDtypeStruct((DEC, W2), BF),
        jax.ShapeDtypeStruct((DEC, W2), BF),
        jax.ShapeDtypeStruct((ROWS, W2), BF),
        jax.ShapeDtypeStruct((ROWS, W2), F32),
        jax.ShapeDtypeStruct((ROWS, W2), F32),
    )
    made = pl.pallas_call(
        kernel,
        out_shape=results,
        in_specs=[any_spec] * 8,
        out_specs=[any_spec] * 5,
        scratch_shapes=[
            pltpu.VMEM((32, 128, 128), BF),
            pltpu.VMEM((32, 128, 128), BF),
            pltpu.VMEM((NZ, W2, W2), BF),
            pltpu.VMEM((NZ, W2, W2), BF),
            pltpu.VMEM((DEC, W2), BF),
            pltpu.VMEM((DEC, W2), BF),
            pltpu.VMEM((ROWS, 2 * W2), F32),
            pltpu.VMEM((NDP * SLOT, ROWS), BF),
            pltpu.VMEM((ROWS, NDP * SLOT), BF),
            pltpu.VMEM((2, NDP * SLOT, W2), BF),
            pltpu.VMEM((2, NDP * SLOT, W2), BF),
            pltpu.VMEM((2, NDP * SLOT, W2), BF),
            pltpu.VMEM((2, NDP * SLOT, W2), BF),
            pltpu.VMEM((2, 2, ROWS, HD), BF),
            pltpu.VMEM((2, 8 * ROWS, HD), BF),
            pltpu.VMEM((8, 8, 128, 128), BF),
            pltpu.VMEM((2, 8, 128, HD), BF),
            pltpu.VMEM((2, 2, 4, 128, HD), BF),
            pltpu.VMEM((NZ, ROWS, W2), F32),
            pltpu.VMEM((2, 4, 4, ROWS, 128), BF),
            pltpu.VMEM((2, 4, 4, ROWS, 128), BF),
            pltpu.VMEM((DEC, W2), BF),
            pltpu.VMEM((DEC, W2), BF),
            pltpu.VMEM((ROWS, W2), BF),
            pltpu.VMEM((2, ROWS, W2), F32),
            pltpu.VMEM((1, NDP), jnp.int32),
            pltpu.VMEM((1, NDP), jnp.int32),
            pltpu.VMEM((1, NDP), jnp.int32),
            dma(()),
            dma((NZ, 2)),
            dma((2,)),
            dma((2, 4, 4)),
            dma((2, 4, 4)),
            dma((NZ,)),
            dma((NZ,)),
            dma((4,)),
            dma((2,)),
            dma((2,)),
            dma((2,)),
            dma((2,)),
            dma((2,)),
            dma((2,)),
            dma((2,)),
            dma((2,)),
            dma((2, 4, 4)),
            dma((2, 4, 4)),
            dma((5,)),
            dma((3,)),
        ],
        compiler_params=pltpu.CompilerParams(
            collective_id=0, has_side_effects=True, vmem_limit_bytes=60 * 1024 * 1024
        ),
    )(queries, enc_rows, key_weight, value_weight, enc_len, dec_len, route, out_grad)
    return pl.pallas_call(
        hand_over,
        out_shape=results,
        in_specs=[any_spec] * 5,
        out_specs=[any_spec] * 5,
        scratch_shapes=[pltpu.VMEM(r.shape, r.dtype) for r in results] + [dma((2, 5))],
        compiler_params=pltpu.CompilerParams(vmem_limit_bytes=60 * 1024 * 1024),
    )(*made)


def solution(mesh):
    in_specs = (
        P("dp", "mp"),
        P("dp", "mp"),
        P(None, "mp"),
        P(None, "mp"),
        P("dp", None),
        P("dp", None),
        P("dp", None),
        P("dp", "mp"),
    )
    out_specs = (P("dp", "mp"), P("dp", "mp"), P("dp", "mp"), P("dp", "mp"), P("dp", "mp"))
    return jax.shard_map(body, mesh=mesh, in_specs=in_specs, out_specs=out_specs, check_vma=False)
```

```python
import jax
import jax.numpy as jnp
from jax import lax
from jax.experimental import pallas as pl
from jax.experimental.pallas import tpu as pltpu
from jax.sharding import PartitionSpec as P

HD = 256
ROWS = 128
DEC = 256
SLOT = 16
NDP = 32
NZ = 8
W2 = 512
FAR = 3
DEAD = 65536.0
FARTHEST_FIRST = (10, 6, 9, 14, 11, 5, 8, 15, 2, 7, 13, 4, 1, 12, 3)
MESH = pl.DeviceIdType.MESH
BF = jnp.bfloat16
F32 = jnp.float32


def mm(a, b):
    return lax.dot_general(a, b, (((1,), (0,)), ((), ())), preferred_element_type=F32)


def mm_nt(a, b):
    return lax.dot_general(a, b, (((1,), (1,)), ((), ())), preferred_element_type=F32)


def mm_tn(a, b):
    return lax.dot_general(a, b, (((0,), (0,)), ((), ())), preferred_element_type=F32)


def iota(shape, dim):
    return lax.broadcasted_iota(jnp.int32, shape, dim)


def column_of(row, n):
    here = iota((n, n), 1)
    there = iota((n, n), 0)
    wide = jnp.broadcast_to(row, (n, n))
    col = jnp.sum(jnp.where(here == there, wide, 0.0), axis=1, keepdims=True)
    before = jnp.sum(jnp.where(here < there, wide, 0.0), axis=1, keepdims=True)
    return col, before


def kernel(
    q_hbm, enc_hbm, kw_hbm, vw_hbm, enc_len_hbm, dec_len_hbm, route_hbm, og_hbm,
    att_hbm, qg_hbm, eg_hbm, kwg_hbm, vwg_hbm,
    e_v, et_v, kw_v, vw_v, q_v, og_v, acc, oh_v, oht_v,
    slots, kvr, gs, gr, gsend, gl, el, ps, cr, dx, rs_s, rs_r,
    att_v, qg_v, eg_v, wg_v, enc_len, dec_len, route,
    enc_sem, w_sem, q_sem, z_send, z_recv, el_send, el_recv, elz_send,
    kv_send, kv_recv, g_send, g_recv, gl_send, gl_recv, c_send, c_recv,
    rs_send, rs_recv, out_sem, int_sem,
):
    d = lax.axis_index("dp")
    z = lax.axis_index("mp")
    x = d // 8
    y = (d // 2) % 4
    c = d % 2
    right = (d, (z + 1) % NZ)
    left = (d, (z + NZ - 1) % NZ)
    ring = (right, left)

    def chunk_at(n):
        off = jnp.where(n % 2 == 1, NZ - (n + 1) // 2, n // 2)
        return (z + off) % NZ

    def drained(buf, sem):
        pltpu.make_async_copy(buf, buf, sem).wait()

    for b in range(4):
        pltpu.make_async_copy(
            enc_hbm.at[:, pl.ds(b * 128, 128)], e_v.at[z * 4 + b], enc_sem
        ).start()

    barrier = pltpu.get_barrier_semaphore()
    for peer in (*ring, (d, (z + 2) % NZ), (d, (z + NZ - 2) % NZ)):
        pl.semaphore_signal(barrier, inc=1, device_id=peer, device_id_type=MESH)

    def greet(i, carry):
        pl.semaphore_signal(barrier, inc=1, device_id=((d + i) % NDP, z), device_id_type=MESH)
        return carry

    lax.fori_loop(1, NDP, greet, 0)

    def w_copy(zc, kv):
        src, dst = ((kw_hbm, kw_v), (vw_hbm, vw_v))[kv]
        return pltpu.make_async_copy(
            src.at[pl.ds(pl.multiple_of(zc * W2, W2), W2), :], dst.at[zc], w_sem.at[zc, kv]
        )

    def load_w(n, carry):
        zc = chunk_at(n)
        w_copy(zc, 0).start()
        w_copy(zc, 1).start()
        return carry

    int_copies = [
        pltpu.make_async_copy(src, dst, int_sem.at[i])
        for i, (src, dst) in enumerate(
            ((enc_len_hbm, enc_len), (route_hbm, route), (dec_len_hbm, dec_len))
        )
    ]
    for copy in int_copies:
        copy.start()

    pl.semaphore_wait(barrier, NDP + 3)
    pltpu.make_async_copy(e_v.at[pl.ds(0, 4)], e_v.at[pl.ds(z * 4, 4)], enc_sem).wait()

    def z_copy(direction, step, part):
        back = step - 1
        zc = (z + NZ - back) % NZ if direction == 0 else (z + back) % NZ
        at = zc * 4 + part
        return pltpu.make_async_remote_copy(
            src_ref=e_v.at[at],
            dst_ref=e_v.at[at],
            send_sem=z_send.at[direction, step - 1, part],
            recv_sem=z_recv.at[direction, step - 1, part],
            device_id=ring[direction],
            device_id_type=MESH,
        )

    def near(direction, part):
        return (part < 2) == (direction == 0)

    travel = ((0, 0), (1, 3), (0, 1), (1, 2), (0, 2), (1, 1), (0, 3), (1, 0))
    for direction, part in travel:
        z_copy(direction, 1, part).start()
    lax.fori_loop(0, NZ, load_w, 0)
    q_copy = pltpu.make_async_copy(q_hbm, q_v, q_sem.at[0])
    og_copy = pltpu.make_async_copy(og_hbm, og_v, q_sem.at[1])
    q_copy.start()
    og_copy.start()

    def to_line(zc, src, dst, device, here):
        @pl.when(here)
        def _():
            pltpu.make_async_copy(src, dst, el_recv.at[zc]).start()

        @pl.when(jnp.logical_not(here))
        def _():
            pltpu.make_async_remote_copy(
                src_ref=src, dst_ref=dst, send_sem=el_send.at[zc], recv_sem=el_recv.at[zc],
                device_id=device, device_id_type=MESH,
            ).start()

    int_copies[0].wait()
    int_copies[1].wait()
    lens_col, starts_col = column_of(enc_len[...].astype(F32), NDP)
    route_col, _ = column_of(route[...].astype(F32), NDP)
    pos = iota((NDP, ROWS), 1).astype(F32)
    inside = (pos >= starts_col) & (pos < starts_col + lens_col)
    dest = jnp.sum(
        jnp.where(inside, route_col * SLOT + pos - starts_col, 0.0), axis=0, keepdims=True
    )
    hot = iota((NDP * SLOT, ROWS), 0).astype(F32) == dest
    hot_f = jnp.where(hot, 1.0, 0.0)
    oh_v[...] = hot_f.astype(BF)

    acc[...] = jnp.zeros_like(acc)

    def process(zc):
        blocks = [e_v[zc * 4 + b] for b in range(4)]
        rows = jnp.concatenate(blocks, axis=1)
        w_copy(zc, 0).wait()
        w_copy(zc, 1).wait()
        acc[:, :W2] += mm(rows, kw_v[zc])
        acc[:, W2:] += mm(rows, vw_v[zc])
        for b in range(4):
            et_v[zc * 4 + b] = blocks[b].T

    def distribute(zc):
        xc = zc // 2
        half = zc % 2
        to_line(
            zc, et_v.at[pl.ds(zc * 4, 4)], el.at[c * 4 + x, pl.ds(half * 4, 4)],
            (xc * 8 + y * 2, z), (xc == x) & (c == 0),
        )
        for j in range(2):
            yc = half * 2 + j
            to_line(
                zc, et_v.at[pl.ds(zc * 4 + 2 * j, 2)], el.at[c * 4 + y, pl.ds(xc * 2, 2)],
                (x * 8 + yc * 2 + 1, z), (yc == y) & (c == 1),
            )

    process(z)
    distribute(z)

    def gather_step(k, carry):
        for direction, part in travel:
            z_copy(direction, k, part).wait_recv()
            if near(direction, part):
                z_copy(direction, k + 1, part).start()
            else:
                pl.when(k < 3)(z_copy(direction, k + 1, part).start)
        for zc in ((z + NZ - k) % NZ, (z + k) % NZ):
            process(zc)
            pl.when(k < FAR)(lambda: distribute(zc))
        return carry

    lax.fori_loop(1, 4, gather_step, 0)
    for direction, part in travel[:4]:
        z_copy(direction, 4, part).wait_recv()
    process((z + 4) % NZ)

    def line_blocks(zc, core):
        return pl.ds((zc % 2) * 4, 4) if core == 0 else pl.ds((zc // 2) * 2, 2)

    def on_holder(zc, fn):
        pl.when((c == 0) & (zc // 2 == x))(lambda: fn(0))
        pl.when((c == 1) & (zc % 2 == y // 2))(lambda: fn(1))

    def wait_line(zc):
        def one(core):
            drained(el.at[:, line_blocks(zc, core)], el_recv.at[zc])

        on_holder(zc, one)

    def along_z(n, act):
        zc, step, first, count = (
            (z + 2, 7, 0, 8), (z + 6, 1, 0, 8), (z + 2, 6, 4, 2), (z + 6, 2, 6, 2),
        )[n]
        zc = zc % NZ

        def one(core):
            at = el.at[pl.ds(first, count), line_blocks(zc, core)]
            act(pltpu.make_async_remote_copy(
                src_ref=at, dst_ref=at, send_sem=elz_send.at[n], recv_sem=el_recv.at[zc],
                device_id=(d, (z + step) % NZ), device_id_type=MESH,
            ))

        on_holder(zc, one)

    def exchange(src, dst, send_sem, recv_sem, h):
        mine = pl.ds(pl.multiple_of(d * SLOT, SLOT), SLOT)
        pltpu.make_async_copy(src.at[h, mine], dst.at[h, mine], recv_sem.at[h]).start()

        def send(i, carry):
            o = jnp.int32(0)
            for n in range(15):
                o = jnp.where(i // 2 == n, FARTHEST_FIRST[n], o)
            t = ((x + o // 4) % 4) * 8 + ((y + o % 4) % 4) * 2 + (c + i + 1) % 2
            pltpu.make_async_remote_copy(
                src_ref=src.at[h, pl.ds(pl.multiple_of(t * SLOT, SLOT), SLOT)],
                dst_ref=dst.at[h, mine],
                send_sem=send_sem.at[h],
                recv_sem=recv_sem.at[h],
                device_id=(t, z),
                device_id_type=MESH,
            ).start()
            return carry

        lax.fori_loop(0, NDP - 1, send, 0)

    most = pl.ds(0, (NDP - 1) * SLOT)
    hot_b = oh_v[...]
    dead = jnp.sum(hot_b.astype(F32), axis=1, keepdims=True) < 0.5
    for h in range(2):
        cols = pl.ds(h * HD, HD)
        keys = mm(hot_b, acc[:, cols].astype(BF))
        slots[h, :, :HD] = jnp.where(dead, DEAD, keys).astype(BF)
        slots[h, :, HD:] = mm(hot_b, acc[:, pl.ds(W2 + h * HD, HD)].astype(BF)).astype(BF)
        exchange(slots, kvr, kv_send, kv_recv, h)

    def relay():
        for k in (2, 6):
            wait_line((z + k) % NZ)
        for n in range(4):
            along_z(n, lambda copy: copy.start())


    relay()
    pl.when(c == 0)(lambda: distribute((z + 4) % NZ))
    oht_v[...] = hot_b.T

    n_keys = NDP * SLOT
    int_copies[2].wait()
    dec_col, dec_before = column_of(dec_len[...].astype(F32), NDP)
    same = iota((NDP, n_keys), 1) // SLOT == iota((NDP, n_keys), 0)
    first = jnp.sum(jnp.where(same, dec_before, 0.0), axis=0, keepdims=True)
    last = jnp.sum(jnp.where(same, dec_before + dec_col, 0.0), axis=0, keepdims=True)
    row = iota((DEC, n_keys), 0).astype(F32)
    own = (row >= first) & (row < last)
    q_copy.wait()
    og_copy.wait()
    for h in range(2):
        cols = pl.ds(h * HD, HD)
        drained(kvr.at[h], kv_recv.at[h])
        q = q_v[:, cols]
        g = og_v[:, cols]
        k = kvr[h, :, :HD]
        v = kvr[h, :, HD:]
        total = mm_nt(jnp.ones((16, HD), BF), k)[:1]
        allowed = own & (total < 4.0e6)
        s = jnp.where(allowed, mm_nt(q, k) * (HD ** -0.5), -1e30)
        top = jnp.max(s, axis=1, keepdims=True)
        expo = jnp.exp(s - top)
        probs = expo * (1.0 / jnp.sum(expo, axis=1, keepdims=True))
        weights = probs.astype(BF)
        dw = mm_nt(g, v)
        delta = jnp.sum(probs * dw, axis=1, keepdims=True)
        ds = (probs * (dw - delta) * (HD ** -0.5)).astype(BF)
        gs[h, :, :HD] = mm_tn(ds, q).astype(BF)
        gs[h, :, HD:] = mm_tn(weights, g).astype(BF)
        exchange(gs, gr, g_send, g_recv, h)
        att_v[:, cols] = mm(weights, v).astype(BF)
        qg_v[:, cols] = mm(ds, k).astype(BF)
    att_out = pltpu.make_async_copy(att_v, att_hbm, out_sem.at[0])
    qg_out = pltpu.make_async_copy(qg_v, qg_hbm, out_sem.at[1])
    att_out.start()
    qg_out.start()

    def spread(h):
        def one(kv, i):
            if kv == 0:
                t = ((x + i) % 4) * 8 + y * 2
                at = c * 4 + x
            else:
                t = x * 8 + ((y + i) % 4) * 2 + 1
                at = c * 4 + y
            src = gsend.at[h, kv]
            dst = gl.at[h, pl.ds(pl.multiple_of(at * ROWS, ROWS), ROWS)]

            def far():
                pltpu.make_async_remote_copy(
                    src_ref=src, dst_ref=dst, send_sem=gl_send.at[h], recv_sem=gl_recv.at[h],
                    device_id=(t, z), device_id_type=MESH,
                ).start()

            if i > 0:
                far()
            else:
                pl.when(c != kv)(far)

                @pl.when(c == kv)
                def _():
                    pltpu.make_async_copy(src, dst, gl_recv.at[h]).start()

        for i in (2, 1, 3, 0):
            one(0, i)
            one(1, i)

    def unpack(h):
        drained(gr.at[h], g_recv.at[h])
        rows = mm(oht_v[...], gr[h]).astype(BF)
        gsend[h, 0] = rows[:, :HD]
        gsend[h, 1] = rows[:, HD:]
        spread(h)

    def back(h, zc):
        cols = pl.ds(h * HD, HD)
        return mm_nt(gsend[h, 0], kw_v[zc, :, cols]) + mm_nt(gsend[h, 1], vw_v[zc, :, cols])

    def send_block(h, b):
        t = jnp.where(c == 0, x * 8 + b, (b // 2) * 8 + y * 2 + b % 2)
        dst = cr.at[h, c, jnp.where(c == 0, y, x)]

        @pl.when(t == d)
        def _():
            pltpu.make_async_copy(ps.at[h, b], dst, c_recv.at[h]).start()

        @pl.when(t != d)
        def _():
            pltpu.make_async_remote_copy(
                src_ref=ps.at[h, b], dst_ref=dst, send_sem=c_send.at[h], recv_sem=c_recv.at[h],
                device_id=(t, z), device_id_type=MESH,
            ).start()

    def partial_blocks(h):
        drained(gl.at[h], gl_recv.at[h])

        def blocks(n, carry):
            lhs = jnp.concatenate(
                [
                    jnp.concatenate([el[j, n * 4 + i] for j in range(8)], axis=1)
                    for i in range(4)
                ],
                axis=0,
            )
            out = mm(lhs, gl[h]).astype(BF)
            for i in range(4):
                ps[h, n * 4 + i] = out[i * 128:(i + 1) * 128]
                send_block(h, n * 4 + i)
            return carry

        lax.fori_loop(0, 2, blocks, 0)

    unpack(0)

    def back_first(zc, carry):
        dx[zc] = back(0, zc)
        return carry

    lax.fori_loop(0, NZ, back_first, 0)
    unpack(1)

    def rs_copy(direction, step, part):
        return pltpu.make_async_remote_copy(
            src_ref=rs_s.at[direction, step - 1, part],
            dst_ref=rs_r.at[direction, step - 1, part],
            send_sem=rs_send.at[direction, step - 1, part],
            recv_sem=rs_recv.at[direction, step - 1, part],
            device_id=ring[direction],
            device_id_type=MESH,
        )

    def rs_part(step, direction, part):
        far = 5 - step
        zc = (z + far) % NZ if direction == 0 else (z + NZ - far) % NZ
        term = dx[zc, :, pl.ds(part * 128, 128)]
        if step >= 3 or (step == 2 and near(direction, part)):
            rs_copy(direction, step - 1, part).wait_recv()
            term = term + rs_r[direction, step - 2, part].astype(F32)
        rs_s[direction, step - 1, part] = term.astype(BF)
        rs_copy(direction, step, part).start()

    def back_second(n, carry):
        zc = chunk_at(7 - n)
        dx[zc] += back(1, zc)
        return carry

    first_parts, last_parts = travel[:4], travel[4:]
    lax.fori_loop(0, 1, back_second, 0)
    for direction, part in first_parts:
        rs_part(1, direction, part)
    lax.fori_loop(1, 3, back_second, 0)
    for direction, part in last_parts:
        rs_part(2, direction, part)
    lax.fori_loop(3, NZ, back_second, 0)
    for k in (0, 1, 7, 3, 5, 4):
        wait_line((z + k) % NZ)
    partial_blocks(0)
    for direction, part in first_parts:
        rs_part(2, direction, part)
    partial_blocks(1)
    for step in (3, 4):
        for direction, part in last_parts + first_parts:
            rs_part(step, direction, part)

    for h in range(2):
        drained(cr.at[h], c_recv.at[h])
        cols = pl.ds(h * HD, HD)
        for kv in range(2):
            total = cr[h, kv, 0].astype(F32)
            for j in range(1, 4):
                total = total + cr[h, kv, j].astype(F32)
            wg_v[kv, :, cols] = total
    kwg_out = pltpu.make_async_copy(wg_v.at[0], kwg_hbm, out_sem.at[2])
    vwg_out = pltpu.make_async_copy(wg_v.at[1], vwg_hbm, out_sem.at[3])
    kwg_out.start()
    vwg_out.start()
    for part in (2, 1, 3, 0):
        cols = pl.ds(part * 128, 128)
        total = dx[z, :, cols]
        for direction in range(2):
            rs_copy(direction, 4, part).wait_recv()
            total = total + rs_r[direction, 3, part].astype(F32)
        eg_v[:, cols] = total.astype(BF)
    eg_out = pltpu.make_async_copy(eg_v, eg_hbm, out_sem.at[4])
    eg_out.start()

    for direction in range(2):
        for step in range(1, 5):
            for part in range(4):
                if step < 4 or near(direction, part):
                    z_copy(direction, step, part).wait_send()
                if step > 1 or near(direction, part):
                    rs_copy(direction, step, part).wait_send()
    for k in (0, 1, 7, 2, 6, 4):
        zc = (z + k) % NZ
        own_x = (c == 0) & (zc // 2 == x)
        own_y = (c == 1) & (zc % 2 == y // 2)
        sent = (c == 0) | (k != 4)
        other = jnp.logical_not(own_x | own_y)
        pl.when(sent & own_x)(lambda: drained(et_v.at[pl.ds(0, 4)], el_send.at[zc]))
        pl.when(sent & own_y)(lambda: drained(et_v.at[pl.ds(0, 6)], el_send.at[zc]))
        pl.when(sent & other)(lambda: drained(et_v.at[pl.ds(0, 8)], el_send.at[zc]))
    for n in range(4):
        along_z(n, lambda copy: copy.wait_send())
    for h in range(2):
        drained(kvr.at[h, most], kv_send.at[h])
        drained(gr.at[h, most], g_send.at[h])
        drained(gl.at[h, pl.ds(0, 7 * ROWS)], gl_send.at[h])
        drained(ps.at[h, pl.ds(0, 7)], c_send.at[h])
    att_out.wait()
    qg_out.wait()
    kwg_out.wait()
    vwg_out.wait()
    eg_out.wait()


def hand_over(*refs):
    given, results, held, sems = refs[:5], refs[5:10], refs[10:15], refs[15]
    inward = [pltpu.make_async_copy(given[i], held[i], sems.at[0, i]) for i in range(5)]
    outward = [pltpu.make_async_copy(held[i], results[i], sems.at[1, i]) for i in range(5)]
    for copy in inward:
        copy.start()
    for i in range(5):
        inward[i].wait()
        outward[i].start()
    for copy in outward:
        copy.wait()


def body(queries, enc_rows, key_weight, value_weight, enc_len, dec_len, route, out_grad):
    any_spec = pl.BlockSpec(memory_space=pl.ANY)
    dma = pltpu.SemaphoreType.DMA
    results = (
        jax.ShapeDtypeStruct((DEC, W2), BF),
        jax.ShapeDtypeStruct((DEC, W2), BF),
        jax.ShapeDtypeStruct((ROWS, W2), BF),
        jax.ShapeDtypeStruct((ROWS, W2), F32),
        jax.ShapeDtypeStruct((ROWS, W2), F32),
    )
    made = pl.pallas_call(
        kernel,
        out_shape=results,
        in_specs=[any_spec] * 8,
        out_specs=[any_spec] * 5,
        scratch_shapes=[
            pltpu.VMEM((32, 128, 128), BF),
            pltpu.VMEM((32, 128, 128), BF),
            pltpu.VMEM((NZ, W2, W2), BF),
            pltpu.VMEM((NZ, W2, W2), BF),
            pltpu.VMEM((DEC, W2), BF),
            pltpu.VMEM((DEC, W2), BF),
            pltpu.VMEM((ROWS, 2 * W2), F32),
            pltpu.VMEM((NDP * SLOT, ROWS), BF),
            pltpu.VMEM((ROWS, NDP * SLOT), BF),
            pltpu.VMEM((2, NDP * SLOT, W2), BF),
            pltpu.VMEM((2, NDP * SLOT, W2), BF),
            pltpu.VMEM((2, NDP * SLOT, W2), BF),
            pltpu.VMEM((2, NDP * SLOT, W2), BF),
            pltpu.VMEM((2, 2, ROWS, HD), BF),
            pltpu.VMEM((2, 8 * ROWS, HD), BF),
            pltpu.VMEM((8, 8, 128, 128), BF),
            pltpu.VMEM((2, 8, 128, HD), BF),
            pltpu.VMEM((2, 2, 4, 128, HD), BF),
            pltpu.VMEM((NZ, ROWS, W2), F32),
            pltpu.VMEM((2, 4, 4, ROWS, 128), BF),
            pltpu.VMEM((2, 4, 4, ROWS, 128), BF),
            pltpu.VMEM((DEC, W2), BF),
            pltpu.VMEM((DEC, W2), BF),
            pltpu.VMEM((ROWS, W2), BF),
            pltpu.VMEM((2, ROWS, W2), F32),
            pltpu.VMEM((1, NDP), jnp.int32),
            pltpu.VMEM((1, NDP), jnp.int32),
            pltpu.VMEM((1, NDP), jnp.int32),
            dma(()),
            dma((NZ, 2)),
            dma((2,)),
            dma((2, 4, 4)),
            dma((2, 4, 4)),
            dma((NZ,)),
            dma((NZ,)),
            dma((4,)),
            dma((2,)),
            dma((2,)),
            dma((2,)),
            dma((2,)),
            dma((2,)),
            dma((2,)),
            dma((2,)),
            dma((2,)),
            dma((2, 4, 4)),
            dma((2, 4, 4)),
            dma((5,)),
            dma((3,)),
        ],
        compiler_params=pltpu.CompilerParams(
            collective_id=0, has_side_effects=True, vmem_limit_bytes=60 * 1024 * 1024
        ),
    )(queries, enc_rows, key_weight, value_weight, enc_len, dec_len, route, out_grad)
    return pl.pallas_call(
        hand_over,
        out_shape=results,
        in_specs=[any_spec] * 5,
        out_specs=[any_spec] * 5,
        scratch_shapes=[pltpu.VMEM(r.shape, r.dtype) for r in results] + [dma((2, 5))],
        compiler_params=pltpu.CompilerParams(vmem_limit_bytes=60 * 1024 * 1024),
    )(*made)


def solution(mesh):
    in_specs = (
        P("dp", "mp"),
        P("dp", "mp"),
        P(None, "mp"),
        P(None, "mp"),
        P("dp", None),
        P("dp", None),
        P("dp", None),
        P("dp", "mp"),
    )
    out_specs = (P("dp", "mp"), P("dp", "mp"), P("dp", "mp"), P("dp", "mp"), P("dp", "mp"))
    return jax.shard_map(body, mesh=mesh, in_specs=in_specs, out_specs=out_specs, check_vma=False)
```
